32 devices in a mesh: grp: 2 (over x), blk: 16 (over z, y, core).
Axes of the slice: x: 2, y: 2, z: 4, core: 2. Of those that a mesh axis runs over, the one named last changes fastest.
Arguments:
- probes: float32 [3, 192, 64, 256], P(None, ('grp', 'blk')), parts along dimension 1, may hold values from -6 to 6
- inverses: float32 [3, 192, 256, 256], P(None, ('grp', 'blk')), parts along dimension 1
- couplings: float32 [2, 192, 4, 256, 256], P(None, ('grp', 'blk')), parts along dimension 1, may hold values from -0.1875 to 0.1875
- neighbour_devices: int32 [2, 192, 4], P(None, 'grp'), parts along dimension 1, may hold values from 0 to 15, all different within a row; in each aligned block of 6 rows (0 to 5, 6 to 11, ..., all dimensions but the last counted through in order) at most 2 rows name the same one
- neighbour_slots: int32 [2, 192, 4], P(None, 'grp'), parts along dimension 1, may hold values from 0 to 5
Outputs:
- solved: float32 [3, 192, 64, 256], P(None, ('grp', 'blk')), parts along dimension 1
The draws below stay inside these ranges and needn't reach their ends.
There are 2 independent parts, one for each index of `grp`. The reference program is written for one: setup_inputs(seed, part) draws one part's arguments, and reference() takes and returns one part's arrays. A program takes and returns all parts, laid end to end along the dimension named above; each array names one. Nothing has to cross between parts.
Inputs may be any that keep to these rules, and one draw needn't show every extreme that they name: `neighbour_devices`: each list names 4 different devices. In each level, the lists of one device's 6 blocks (aligned blocks of 6 rows) name no device more than 2 times, and some device exactly 2 times.
All inputs are finite; a program needn't handle non-finite values.
Results may differ from the reference program's by a relative error of at most 0.0001.
Values sent between devices are 32-bit elements; how exact they have to be, the bound alone decides.
No kernel may reach another device: no remote copies, remote signals or barrier semaphores. Data moves between devices by JAX's collectives and lax.ppermute only.
A program may use at most 128 MiB of HBM per device.

```python
import math
import jax
import jax.numpy as jnp
import numpy as np
from jax import lax

BS = 256
P_SIZE = 64
K = 4
LEVELS = 3
PER = 6
CAP = 2
NBLK_L = 96
N_BLK = 16


def draw_inverses(key, part):
    key = jax.random.fold_in(key, 11)
    first_key, second_key = jax.random.split(key)
    eye_matrix = jnp.eye(BS, dtype=jnp.float32)
    diagonal = jax.random.uniform(second_key, (LEVELS, NBLK_L, BS, 1), jnp.float32, 0.6, 1.2)
    noise = jnp.clip(jax.random.normal(first_key, (LEVELS, NBLK_L, BS, BS), jnp.float32), -3.0, 3.0) * (0.3 / BS ** 0.5)
    return diagonal * eye_matrix + noise


def place_ends(entries, stream_key, least, largest):
    extent = entries.shape
    spot = [jax.random.randint(jax.random.fold_in(stream_key, axis), (), 0, extent[axis]) for axis in range(len(extent))]
    entries = entries.at[tuple(spot)].set(least)
    longest = extent.index(max(extent))
    spot[longest] = (spot[longest] + 1) % extent[longest]
    return entries.at[tuple(spot)].set(largest)


def levels(key, dims, cuts, low, high):
    loudness, own = 1.0, jax.random.fold_in(key, 6)
    for position, parts in cuts:
        draws = jnp.exp(jax.random.uniform(jax.random.fold_in(own, position), (parts,), jnp.float32, low / len(cuts), high / len(cuts)))
        loudness = loudness * jnp.repeat(draws, dims[position] // parts).reshape([-1 if axis == position else 1 for axis in range(len(dims))])
    return loudness


def shared_out(own_key, own, number, rows, count, top, reach, slope):
    sequence = jax.random.permutation(own_key, count)
    crowded, usual = portions_of(count, rows * top, reach, slope, True), portions_of(count, rows * top, reach, slope, False)
    places = jnp.arange(count)

    def named(tallies, turn):
        used = int((tallies > 0).sum())
        fixed = max(1, used // 4)
        passed = fixed + (places - fixed + turn * (used - fixed)) % max(1, count - fixed)
        return jnp.zeros((count,), jnp.int32).at[sequence[jnp.where(places < fixed, places, passed)]].set(jnp.asarray(tallies, jnp.int32))

    tallies = jnp.where(number % 4 == 0, named(crowded, number // 4), named(usual, number - number // 4 - 1))
    mixed = jax.random.permutation(jax.random.fold_in(own, 3), count)
    donor, taker = mixed[0:count // 2 * 2:2], mixed[1:count // 2 * 2:2]
    room = jnp.minimum(tallies[donor] - 1, reach - tallies[taker]) // 2
    room = jnp.where((donor == sequence[0]) | (taker == sequence[0]) | (tallies[taker] == 0), 0, jnp.maximum(room, 0))
    passed = jax.random.randint(jax.random.fold_in(own, 4), (count // 2,), 0, 1 << 20) % (room + 1)
    tallies = tallies.at[donor].add(-passed).at[taker].add(passed)
    members = jnp.searchsorted(jnp.cumsum(tallies), jnp.arange(rows * top), side="right").astype(jnp.int32)
    listing = members.reshape(top, rows).T
    listing = listing[jax.random.permutation(jax.random.fold_in(own, 1), rows)]
    turn = jax.random.randint(jax.random.fold_in(own, 2), (rows, 1), 0, top)
    return jnp.take_along_axis(listing, (jnp.arange(top)[None, :] + turn) % top, axis=1)


def portions_of(number_of, total, most, lean, full):
    loads = [(1 << 20) // math.isqrt(rank ** lean) + 1 for rank in range(1, number_of + 1)]
    largest = most if full else min(most, max(-(-total // number_of), total * loads[0] // sum(loads)))
    least = 1 if total - largest >= number_of - 1 else 0
    holding, spare = [largest] + [least] * (number_of - 1), total - largest - least * (number_of - 1)
    while spare > 0:
        candidates = [i for i in range(1, number_of) if holding[i] < largest] or [i for i in range(1, number_of) if holding[i] < most]
        pool, left = sum([loads[i] for i in candidates]), spare
        for i in candidates:
            addition = min(most - holding[i], max(1, left * loads[i] // pool), spare)
            holding[i] = holding[i] + addition
            spare = spare - addition
    return np.array(holding)


def centred(stream_key, dims, deviation, limit, pieces=(), kind=jnp.bfloat16):
    array = deviation * jax.random.normal(stream_key, dims, jnp.float32)
    if pieces:
        array = array * levels(stream_key, dims, pieces, -0.22, 0.18)
    return jnp.clip(array, -limit, limit).astype(kind)


def setup_inputs(seed: int = 0, part: int = 0) -> dict:
    streams_of = jax.random.split(jax.random.key(seed), 6)
    part_splits = jax.random.split(jax.random.fold_in(streams_of[5], part), 6)
    probes = centred(part_splits[0], (LEVELS, NBLK_L, P_SIZE, BS), 1.0, 6.0, ((1, 16),), jnp.float32)
    inverses = draw_inverses(jax.random.fold_in(jax.random.fold_in(streams_of[5], part), 71), part)
    couplings = centred(part_splits[2], (LEVELS - 1, NBLK_L, K, BS, BS), (K * BS) ** -0.5, 0.1875, ((1, 16),), jnp.float32)
    neighbour_devices_keys = jax.random.split(jax.random.fold_in(part_splits[3], 1), (LEVELS - 1) * NBLK_L // PER)
    neighbour_devices_turns = jax.random.permutation(jax.random.fold_in(part_splits[3], 3), (LEVELS - 1) * NBLK_L // PER)
    neighbour_devices = jax.vmap(lambda own, number: shared_out(jax.random.fold_in(part_splits[3], 2), own, number, PER, N_BLK, K, CAP, 2))(neighbour_devices_keys, neighbour_devices_turns).reshape((LEVELS - 1, NBLK_L, K))
    neighbour_slots = place_ends(jax.random.randint(part_splits[4], (LEVELS - 1, NBLK_L, K), 0, PER), jax.random.fold_in(part_splits[4], 1), 0, PER - 1).astype(jnp.int32)
    return dict(probes=probes, inverses=inverses, couplings=couplings, neighbour_devices=neighbour_devices, neighbour_slots=neighbour_slots)


def solve_right(panel, inverse):
    return jnp.einsum("bpi,bji->bpj", panel, inverse, precision=lax.Precision.HIGHEST)


def solve_left(panel, inverse):
    return jnp.einsum("bpj,bji->bpi", panel, inverse, precision=lax.Precision.HIGHEST)


def reference(probes, inverses, couplings, neighbour_devices, neighbour_slots):
    forward = [solve_right(probes[0], inverses[0])]
    for height in range(1, LEVELS):
        source = (neighbour_devices[height - 1] * PER + neighbour_slots[height - 1]).astype(jnp.int32)
        fetched = forward[-1][source]
        coupled = jnp.einsum("bkpi,bkji->bpj", fetched, couplings[height - 1], precision=lax.Precision.HIGHEST)
        forward.append(solve_right(probes[height] - coupled, inverses[height]))
    solved = [None] * LEVELS
    solved[LEVELS - 1] = solve_left(forward[LEVELS - 1], inverses[LEVELS - 1])
    for height in range(LEVELS - 2, -1, -1):
        source = (neighbour_devices[height] * PER + neighbour_slots[height]).astype(jnp.int32)
        partials = jnp.einsum("bpj,bkji->bkpi", solved[height + 1], couplings[height], precision=lax.Precision.HIGHEST)
        incoming = jnp.zeros((NBLK_L, P_SIZE, BS), jnp.float32).at[source.reshape(-1)].add(partials.reshape(-1, P_SIZE, BS))
        solved[height] = solve_left(forward[height] - incoming, inverses[height])
    return jnp.stack(solved)
```

```python
import functools

import jax
import jax.numpy as jnp
from jax import lax
from jax.experimental import pallas as pl
from jax.experimental.pallas import tpu as pltpu
from jax.sharding import PartitionSpec as P

LEVELS = 3
CAP = 2
PLANE = 4
CHUNKS = 2
F32 = jnp.float32
BF16 = jnp.bfloat16
NT = (((1,), (1,)), ((), ()))
NN = (((1,), (0,)), ((), ()))
PARAMS = pltpu.CompilerParams(vmem_limit_bytes=32 * 1024 * 1024)


def low_bit(offset):
    return offset & -offset


def near(offset):
    return offset & (offset - 1) == 0


def split(value):
    high = value.astype(BF16)
    return high, (value - high.astype(F32)).astype(BF16)


def product(panel, matrix, dims):
    rows = panel.shape[0]
    panel_high, panel_low = split(panel)
    matrix_high, matrix_low = split(matrix)
    both = lax.dot_general(
        jnp.concatenate([panel_high, panel_low], axis=0), matrix_high, dims, preferred_element_type=F32
    )
    cross = lax.dot_general(panel_high, matrix_low, dims, preferred_element_type=F32)
    return both[:rows] + (both[rows:] + cross)


def tables(dev_rows, slot_rows, members, position):
    levels, rows, fanout = dev_rows.shape
    blocks_dev = rows // members
    width = blocks_dev * fanout
    depth = members // PLANE
    height, place = position // PLANE, position % PLANE
    start = height * PLANE
    flips = jnp.arange(PLANE)
    offsets = jnp.arange(depth)

    def plane_rows(table):
        table = table.reshape(levels, members, width)
        return lax.dynamic_slice_in_dim(table, start, PLANE, axis=1)

    lists, slots = plane_rows(dev_rows), plane_rows(slot_rows)
    positions = jnp.arange(width)
    earlier = positions[None, :] < positions[:, None]
    matches = lists[:, :, :, None] == lists[:, :, None, :]
    rank = jnp.sum(jnp.logical_and(matches, earlier), axis=3, dtype=jnp.int32)
    code = lists * CAP + rank
    owners = (height ^ offsets) * PLANE + place
    wanted = (owners[:, None] * CAP + jnp.arange(CAP)[None, :]).reshape(depth * CAP)
    found = code[:, :, None, :] == wanted[None, None, :, None]
    by_place = jnp.sum(jnp.where(found, slots[:, :, None, :] + 1, 0), axis=3) - 1
    pick = (flips[:, None] ^ place) == flips[None, :]
    packed = jnp.sum(jnp.where(pick[None, :, :, None], by_place[:, None], 0), axis=2)
    mine = (flips == place)[None, :, None]
    own_dev = jnp.sum(jnp.where(mine, lists, 0), axis=1)
    own_slot = jnp.sum(jnp.where(mine, slots, 0), axis=1)
    own_rank = jnp.sum(jnp.where(mine, rank, 0), axis=1)
    flip = (own_dev % PLANE) ^ place
    offset = (own_dev // PLANE) ^ height
    fetch = jnp.where(
        flip == 0,
        offset * blocks_dev + own_slot,
        depth * blocks_dev + ((flip - 1) * depth + offset) * CAP + own_rank,
    )
    put = (flip * depth + offset) * CAP + own_rank
    return packed.reshape(levels, PLANE * depth * CAP), fetch, put


def whole_spec(array):
    return pl.BlockSpec(array.shape, lambda *_: (0,) * array.ndim)


def solve_kernel(*refs, has_fetch, has_probe, has_left, has_parts, order, depth, blocks, fanout):
    refs = list(refs)
    fetch_ref = refs.pop(0)
    put_ref = refs.pop(0)
    probe_ref = refs.pop(0)
    inverse_ref = refs.pop(0)
    coupling_ref = refs.pop(0) if has_fetch or has_parts else None
    step = pl.program_id(0)
    sums = []
    if has_fetch:
        local_refs = [refs.pop(0) for _ in range(depth)]
        moved_refs = [refs.pop(0) for _ in range(2 * (PLANE - 1))]
    elif not has_probe:
        sums = [refs.pop(0) for _ in range(1 + depth.bit_length() - 1)]
    forward_ref = refs.pop(0) if not has_left else None
    solved_ref = refs.pop(0) if has_left else None
    part_refs = [refs.pop(0) for _ in range(2 * PLANE)] if has_parts else []
    pan_ref = refs.pop(0) if has_fetch else None
    hold_ref = refs.pop(0) if has_parts else None
    if has_fetch:

        @pl.when(step == 0)
        def _():
            for offset in range(depth):
                pan_ref[pl.ds(offset * blocks, blocks)] = local_refs[offset][...]
            for flip in range(PLANE - 1):
                for group in range(2):
                    for place, offset in enumerate(order[group]):
                        base = depth * blocks + (flip * depth + offset) * CAP
                        pan_ref[pl.ds(base, CAP)] = moved_refs[group * (PLANE - 1) + flip][place]

    value = probe_ref[...]
    if has_fetch:
        for k in range(fanout):
            value = value - product(pan_ref[fetch_ref[step * fanout + k]], coupling_ref[k], NT)
    for ref in sums:
        value = value - ref[step]
    if has_probe:
        value = product(value, inverse_ref[...], NT)
    if has_left:
        value = product(value, inverse_ref[...], NN)
        solved_ref[...] = value
    else:
        forward_ref[...] = value
    if has_parts:
        for k in range(fanout):
            hold_ref[put_ref[step * fanout + k]] = product(value, coupling_ref[k], NN)

        @pl.when(step == blocks - 1)
        def _():
            for flip in range(PLANE):
                for group in range(2):
                    for place, offset in enumerate(order[group]):
                        part_refs[group * PLANE + flip][place] = hold_ref[pl.ds((flip * depth + offset) * CAP, CAP)]


def solve(
    fetch, put, panel, panel_level, inverses, couplings, level, chunk, order, depth,
    local=None, moved=None, sums=None, left=False, coupling_level=None,
):
    blocks, points = inverses.shape[1], inverses.shape[3]
    fanout = couplings.shape[2]
    has_probe = panel_level is not None
    rows = panel.shape[2] // CHUNKS if has_probe else panel.shape[1]
    has_fetch = local is not None
    has_parts = left and coupling_level is not None
    block_spec = pl.BlockSpec((None, rows, points), lambda g, *_: (g, 0, 0))
    operands, specs = [panel], []
    if has_probe:
        specs.append(pl.BlockSpec((None, None, rows, points), lambda g, *_: (panel_level, g, chunk, 0)))
    else:
        specs.append(block_spec)
    operands.append(inverses)
    specs.append(pl.BlockSpec((None, None, points, points), lambda g, *_: (level, g, 0, 0)))
    if has_fetch or has_parts:
        operands.append(couplings)
        specs.append(
            pl.BlockSpec((None, None, fanout, points, points), lambda g, *_: (coupling_level, g, 0, 0, 0))
        )
    if has_fetch:
        extra = list(local) + list(moved)
    else:
        extra = list(sums) if sums is not None else []
    operands += extra
    specs += [whole_spec(array) for array in extra]
    out_shapes = [jax.ShapeDtypeStruct((blocks, rows, points), F32)]
    out_specs = [block_spec]
    scratch = []
    if has_fetch:
        scratch.append(pltpu.VMEM((depth * (blocks + (PLANE - 1) * CAP), rows, points), F32))
    if has_parts:
        for group in range(2):
            for _ in range(PLANE):
                shape = jax.ShapeDtypeStruct((len(order[group]), CAP, rows, points), F32)
                out_shapes.append(shape)
                out_specs.append(whole_spec(shape))
        scratch.append(pltpu.VMEM((PLANE * depth * CAP, rows, points), F32))
    kernel = functools.partial(
        solve_kernel, has_fetch=has_fetch, has_probe=has_probe, has_left=left, has_parts=has_parts,
        order=order, depth=depth, blocks=blocks, fanout=fanout,
    )
    return pl.pallas_call(
        kernel,
        out_shape=out_shapes,
        grid_spec=pltpu.PrefetchScalarGridSpec(
            num_scalar_prefetch=2, grid=(blocks,), in_specs=specs, out_specs=out_specs, scratch_shapes=scratch
        ),
        compiler_params=PARAMS,
    )(fetch, put, *operands)


def pack_kernel(packed_ref, *refs, offsets, depth):
    sources = refs[: len(offsets)]
    targets = refs[len(offsets) : len(offsets) + PLANE - 1]
    sems = refs[-1]
    copies = []
    for flip in range(1, PLANE):
        for place, offset in enumerate(offsets):
            for rank in range(CAP):
                slot = jnp.maximum(packed_ref[(flip * depth + offset) * CAP + rank], 0)
                copies.append(
                    pltpu.make_async_copy(
                        sources[place].at[slot], targets[flip - 1].at[place, rank], sems.at[len(copies)]
                    )
                )
                copies[-1].start()
    for copy in copies:
        copy.wait()


def pack(packed, sources, offsets, depth):
    rows, points = sources[0].shape[1:]
    count = (PLANE - 1) * len(offsets) * CAP
    anywhere = pl.BlockSpec(memory_space=pl.ANY)
    return pl.pallas_call(
        functools.partial(pack_kernel, offsets=offsets, depth=depth),
        out_shape=[jax.ShapeDtypeStruct((len(offsets), CAP, rows, points), F32)] * (PLANE - 1),
        grid_spec=pltpu.PrefetchScalarGridSpec(
            num_scalar_prefetch=1,
            grid=(),
            in_specs=[anywhere] * len(offsets),
            out_specs=[anywhere] * (PLANE - 1),
            scratch_shapes=[pltpu.SemaphoreType.DMA((count,))],
        ),
        compiler_params=PARAMS,
    )(packed, *sources)


def gather_kernel(packed_ref, *refs, offsets, depth, extra):
    sources = refs[:PLANE]
    extras = refs[PLANE : PLANE + len(extra)]
    targets = refs[PLANE + len(extra) :]
    for place, offset in enumerate(offsets):
        start = jnp.zeros(targets[place].shape, F32)
        for ref, to in zip(extras, extra):
            if to == offset:
                start = start + ref[...]
        targets[place][...] = start
    for flip in range(PLANE):
        for place, offset in enumerate(offsets):
            for rank in range(CAP):
                slot = packed_ref[(flip * depth + offset) * CAP + rank]

                @pl.when(slot >= 0)
                def _(place=place, flip=flip, rank=rank, slot=slot):
                    targets[place][slot] = targets[place][slot] + sources[flip][place, rank]


def gather_sums(packed, sources, offsets, depth, blocks, extra):
    rows, points = sources[0].shape[2:]
    operands = list(sources) + [array for _, array in extra]
    shape = jax.ShapeDtypeStruct((blocks, rows, points), F32)
    return pl.pallas_call(
        functools.partial(gather_kernel, offsets=offsets, depth=depth, extra=[to for to, _ in extra]),
        out_shape=[shape] * len(offsets),
        grid_spec=pltpu.PrefetchScalarGridSpec(
            num_scalar_prefetch=1,
            grid=(1,),
            in_specs=[whole_spec(array) for array in operands],
            out_specs=[whole_spec(shape)] * len(offsets),
        ),
        compiler_params=PARAMS,
    )(packed, *operands)


def flip_move(array, bits):
    members = lax.axis_size("blk")
    return lax.ppermute(array, "blk", [(source, source ^ bits) for source in range(members)])


def local(probes, inverses, couplings, neighbour_devices, neighbour_slots):
    members = lax.axis_size("blk")
    position = lax.axis_index("blk")
    blocks = probes.shape[1]
    depth = members // PLANE
    packed, fetch, put = tables(neighbour_devices, neighbour_slots, members, position)
    order = (
        tuple(offset for offset in range(depth) if near(offset)),
        tuple(offset for offset in range(depth) if not near(offset)),
    )
    far_first = sorted(order[1], key=lambda offset: -offset.bit_count())
    call = functools.partial(solve, inverses=inverses, couplings=couplings, order=order, depth=depth)

    def spread(panels, level):
        held = {0: panels}
        for offset in sorted(order[0][1:], reverse=True):
            held[offset] = flip_move(panels, offset * PLANE)
        for offset in sorted(order[1], key=lambda offset: offset.bit_count()):
            held[offset] = flip_move(held[offset ^ low_bit(offset)], low_bit(offset) * PLANE)
        moved = []
        for group in order:
            packs = pack(packed[level], [held[offset] for offset in group], group, depth)
            moved += [flip_move(array, flip + 1) for flip, array in enumerate(packs)]
        return [held[offset] for offset in range(depth)], moved

    def collect(parts, level):
        arrived = []
        sums = {}
        for group in (1, 0):
            own = parts[group * PLANE]
            others = [flip_move(parts[group * PLANE + flip], flip) for flip in range(1, PLANE)]
            extra = [entry for entry in arrived if entry[0] in order[0][1:]] if group == 0 else []
            results = gather_sums(packed[level], [own] + others, order[group], depth, blocks, extra)
            sums.update(zip(order[group], results))
            if group == 1:
                for offset in far_first:
                    total = sums[offset]
                    for to, array in arrived:
                        if to == offset:
                            total = total + array
                    bit = low_bit(offset)
                    arrived.append((offset ^ bit, flip_move(total, bit * PLANE)))
        addends = [sums[0]]
        for offset in sorted(order[0][1:], reverse=True):
            addends.append(flip_move(sums[offset], offset * PLANE))
        return addends

    columns = []
    for chunk in range(CHUNKS):
        forward = []
        solved = [None] * LEVELS
        (panels,) = call(fetch[0], put[0], probes, 0, level=0, chunk=chunk)
        forward.append(panels)
        for level in range(1, LEVELS):
            held, moved = spread(forward[-1], level - 1)
            top = level == LEVELS - 1
            results = call(
                fetch[level - 1], put[level - 1], probes, level, level=level, chunk=chunk,
                local=held, moved=moved, left=top, coupling_level=level - 1,
            )
            if top:
                solved[level], parts = results[0], results[1:]
            else:
                forward.append(results[0])
        for level in range(LEVELS - 2, -1, -1):
            addends = collect(parts, level)
            lower = level - 1 if level else None
            results = call(
                fetch[max(level - 1, 0)], put[max(level - 1, 0)], forward[level], None, level=level, chunk=chunk,
                sums=addends, left=True, coupling_level=lower,
            )
            solved[level], parts = results[0], results[1:]
        columns.append(jnp.stack(solved))
    return jnp.concatenate(columns, axis=2)


def solution(mesh):
    return jax.shard_map(
        local,
        mesh=mesh,
        in_specs=(
            P(None, ("grp", "blk"), None, None),
            P(None, ("grp", "blk"), None, None),
            P(None, ("grp", "blk"), None, None, None),
            P(None, "grp", None),
            P(None, "grp", None),
        ),
        out_specs=P(None, ("grp", "blk"), None, None),
        check_vma=False,
    )
```

```python
import functools

import jax
import jax.numpy as jnp
from jax import lax
from jax.experimental import pallas as pl
from jax.experimental.pallas import tpu as pltpu
from jax.sharding import PartitionSpec as P

LEVELS = 3
CAP = 2
PLANE = 4
CHUNKS = 2
F32 = jnp.float32
BF16 = jnp.bfloat16
NT = (((1,), (1,)), ((), ()))
NN = (((1,), (0,)), ((), ()))
PARAMS = pltpu.CompilerParams(vmem_limit_bytes=16 * 1024 * 1024)


def low_bit(offset):
    return offset & -offset


def split(value):
    high = value.astype(BF16)
    return high, (value - high.astype(F32)).astype(BF16)


def product(panel, high, low, dims):
    rows = panel.shape[0]
    panel_high, panel_low = split(panel)
    both = lax.dot_general(
        jnp.concatenate([panel_high, panel_low], axis=0), high, dims, preferred_element_type=F32
    )
    cross = lax.dot_general(panel_high, low, dims, preferred_element_type=F32)
    return both[:rows] + (both[rows:] + cross)


def line_offsets(depth):
    whole = tuple(offset for offset in range(depth) if offset % 2 == 0 or offset == 1)
    return whole, tuple(offset for offset in range(depth) if offset not in whole)


def lookup(values, index):
    hits = index[..., None] == jnp.arange(len(values))
    return jnp.sum(jnp.where(hits, jnp.array(values, jnp.int32), 0), axis=-1)


def tables(dev_rows, slot_rows, members, position):
    levels, rows, fanout = dev_rows.shape
    blocks_dev = rows // members
    width = blocks_dev * fanout
    depth = members // PLANE
    whole, listed = line_offsets(depth)
    height, place = position // PLANE, position % PLANE
    flips = jnp.arange(PLANE)

    def plane_rows(table, at):
        table = table.reshape(levels, members, width)
        return lax.dynamic_slice_in_dim(table, at * PLANE, PLANE, axis=1)

    lists = jnp.stack([plane_rows(dev_rows, height), plane_rows(dev_rows, height ^ 1)])
    slots = jnp.stack([plane_rows(slot_rows, height), plane_rows(slot_rows, height ^ 1)])
    positions = jnp.arange(width)
    earlier = positions[None, :] < positions[:, None]
    matches = lists[..., :, None] == lists[..., None, :]
    rank = jnp.sum(jnp.logical_and(matches, earlier), axis=-1, dtype=jnp.int32)
    code = lists * CAP + rank
    pick = (flips[:, None] ^ place) == flips[None, :]

    def asked(readers, offsets):
        owners = (height ^ jnp.array(offsets, jnp.int32)) * PLANE + place
        wanted = (owners[:, None] * CAP + jnp.arange(CAP)[None, :]).reshape(len(offsets) * CAP)
        found = code[readers][:, :, None, :] == wanted[None, None, :, None]
        by_place = jnp.sum(jnp.where(found, slots[readers][:, :, None, :] + 1, 0), axis=3) - 1
        by_flip = jnp.sum(jnp.where(pick[None, :, :, None], by_place[:, None], 0), axis=2)
        return by_flip.reshape(levels, PLANE * len(offsets) * CAP)

    plane = asked(0, whole)
    beyond = asked(1, tuple(offset ^ 1 for offset in listed))
    mine = (flips == place)[None, :, None]
    own_dev = jnp.sum(jnp.where(mine, lists[0], 0), axis=1)
    own_slot = jnp.sum(jnp.where(mine, slots[0], 0), axis=1)
    own_rank = jnp.sum(jnp.where(mine, rank[0], 0), axis=1)
    flip = (own_dev % PLANE) ^ place
    offset = (own_dev // PLANE) ^ height
    spot = lookup([whole.index(o) if o in whole else listed.index(o) for o in range(depth)], offset)
    is_whole = lookup([int(o in whole) for o in range(depth)], offset) == 1
    moved = len(whole) * blocks_dev
    far = moved + (PLANE - 1) * len(whole) * CAP
    fetch = jnp.where(
        is_whole,
        jnp.where(
            flip == 0,
            spot * blocks_dev + own_slot,
            moved + ((flip - 1) * len(whole) + spot) * CAP + own_rank,
        ),
        far + (flip * len(listed) + spot) * CAP + own_rank,
    )
    put = (flip * depth + offset) * CAP + own_rank
    return plane, beyond, fetch, put


VMEM_SPEC = pl.BlockSpec(memory_space=pltpu.VMEM)


def halves_kernel(*refs, streams, count):
    step = pl.program_id(0)
    for stream in range(streams):
        high, low = split(refs[stream][...])
        refs[streams][pl.ds((stream * count + step) * high.shape[0], high.shape[0])] = high
        refs[streams + 1][pl.ds((stream * count + step) * high.shape[0], high.shape[0])] = low


def halves(matrices, level, streams, width):
    points = matrices.shape[-1]
    matrices = matrices.reshape(matrices.shape[0], -1, points, points)
    total = matrices.shape[1]
    count = total // (streams * width)
    shape = pltpu.VMEM((total, points, points), BF16)
    specs = [
        pl.BlockSpec((None, width, points, points), lambda step, stream=stream: (level, stream * count + step, 0, 0))
        for stream in range(streams)
    ]
    return pl.pallas_call(
        functools.partial(halves_kernel, streams=streams, count=count),
        out_shape=[shape, shape],
        grid=(count,),
        in_specs=specs,
        out_specs=[VMEM_SPEC, VMEM_SPEC],
        compiler_params=PARAMS,
    )(*[pltpu.with_memory_space_constraint(matrices, pltpu.HBM)] * streams)


def first_kernel(probe_ref, inverse_ref, forward_ref):
    forward_ref[...] = product(probe_ref[...], *split(inverse_ref[...]), NT)


def first(probes, inverses, chunk):
    blocks, rows, points = probes.shape[1], probes.shape[2] // CHUNKS, probes.shape[3]
    return pl.pallas_call(
        first_kernel,
        out_shape=jax.ShapeDtypeStruct((blocks, rows, points), F32),
        grid=(blocks,),
        in_specs=[
            pl.BlockSpec((None, None, rows, points), lambda g: (0, g, chunk, 0)),
            pl.BlockSpec((None, None, points, points), lambda g: (0, g, 0, 0)),
        ],
        out_specs=pl.BlockSpec((None, rows, points), lambda g: (g, 0, 0)),
        compiler_params=PARAMS,
    )(*[pltpu.with_memory_space_constraint(array, pltpu.HBM) for array in (probes, inverses)])


def solve_kernel(*refs, has_fetch, has_left, has_parts, whole, listed, blocks, fanout, adds):
    refs = list(refs)

    def take(count):
        taken, refs[:count] = refs[:count], []
        return taken

    fetch_ref, put_ref, panel_ref = take(3)
    inverse_refs = take(2)
    in_refs = take(2) if has_fetch else None
    back_refs = (in_refs if has_fetch else take(2)) if has_parts else None
    sums = []
    if has_fetch:
        local_refs = take(len(whole))
        moved_refs = take(PLANE - 1)
        far_refs = take(PLANE)
    else:
        sums = take(adds)
    (out_ref,) = take(1)
    if has_parts:
        near_parts, far_parts = take(PLANE), take(PLANE)
    pan_ref = take(1)[0] if has_fetch else None
    hold_ref = take(1)[0] if has_parts else None
    if has_fetch:
        start = 0
        for ref in local_refs:
            pan_ref[pl.ds(start, blocks)] = ref[...]
            start += blocks
        for ref, offsets in [(ref, whole) for ref in moved_refs] + [(ref, listed) for ref in far_refs]:
            for place in range(len(offsets)):
                pan_ref[pl.ds(start, CAP)] = ref[place]
                start += CAP

    for g in range(blocks):
        inverse = [ref[g] for ref in inverse_refs]
        if has_fetch:
            value = panel_ref[g]
            for k in range(fanout):
                coupling = [ref[g * fanout + k] for ref in in_refs]
                value = value - product(pan_ref[fetch_ref[g * fanout + k]], *coupling, NT)
            value = product(value, *inverse, NT)
        else:
            value = panel_ref[g]
            for ref in sums:
                value = value - ref[g]
        if has_left:
            value = product(value, *inverse, NN)
        out_ref[g] = value
        if has_parts:
            for k in range(fanout):
                coupling = [ref[g * fanout + k] for ref in back_refs]
                hold_ref[put_ref[g * fanout + k]] = product(value, *coupling, NN)

    if has_parts:
        depth = len(whole) + len(listed)
        for flip in range(PLANE):
            for part_refs, offsets in ((near_parts, whole), (far_parts, listed)):
                for place, offset in enumerate(offsets):
                    part_refs[flip][place] = hold_ref[pl.ds((flip * depth + offset) * CAP, CAP)]


def solve(fetch, put, panel, inverse, coupling, whole, listed, held=None, moved=None, far=None, sums=None, left=False):
    blocks, rows, points = panel.shape
    has_fetch = held is not None
    has_parts = left and coupling is not None
    fanout = coupling[0].shape[0] // blocks if coupling is not None else 0
    operands = [panel, *inverse, *(coupling if coupling is not None else [])]
    operands = [operands[0]] + [pltpu.with_memory_space_constraint(array, pltpu.VMEM) for array in operands[1:]]
    operands += [*held, *moved, *far] if has_fetch else sums
    out_shapes = [jax.ShapeDtypeStruct((blocks, rows, points), F32)]
    scratch = []
    if has_fetch:
        slots = len(whole) * blocks + ((PLANE - 1) * len(whole) + PLANE * len(listed)) * CAP
        scratch.append(pltpu.VMEM((slots, rows, points), F32))
    if has_parts:
        for offsets in (whole, listed):
            out_shapes += [jax.ShapeDtypeStruct((len(offsets), CAP, rows, points), F32)] * PLANE
        scratch.append(pltpu.VMEM((PLANE * (len(whole) + len(listed)) * CAP, rows, points), F32))
    kernel = functools.partial(
        solve_kernel, has_fetch=has_fetch, has_left=left, has_parts=has_parts, whole=whole, listed=listed,
        blocks=blocks, fanout=fanout, adds=0 if has_fetch else len(sums),
    )
    results = pl.pallas_call(
        kernel,
        out_shape=out_shapes,
        grid_spec=pltpu.PrefetchScalarGridSpec(
            num_scalar_prefetch=2, grid=(), in_specs=[VMEM_SPEC] * len(operands),
            out_specs=[VMEM_SPEC] * len(out_shapes), scratch_shapes=scratch,
        ),
        compiler_params=PARAMS,
    )(fetch, put, *operands)
    return results[0], results[1 : 1 + PLANE], results[1 + PLANE :]


def pack_kernel(plane_ref, beyond_ref, *refs, whole, listed):
    sources = dict(zip(whole, refs))
    moved, far = refs[len(whole) : len(whole) + PLANE - 1], refs[len(whole) + PLANE - 1 :]

    def copy(table_ref, row, target, place, rank, source):
        slot = jnp.maximum(table_ref[row * CAP + rank], 0)
        target[place, rank] = source[slot]

    for flip in range(PLANE):
        for rank in range(CAP):
            for place, offset in enumerate(whole):
                if flip:
                    copy(plane_ref, flip * len(whole) + place, moved[flip - 1], place, rank, sources[offset])
            for place, offset in enumerate(listed):
                copy(beyond_ref, flip * len(listed) + place, far[flip], place, rank, sources[offset ^ 1])


def pack(plane, beyond, held, whole, listed):
    rows, points = held[0].shape[1:]
    near_shape = jax.ShapeDtypeStruct((len(whole), CAP, rows, points), F32)
    far_shape = jax.ShapeDtypeStruct((len(listed), CAP, rows, points), F32)
    results = pl.pallas_call(
        functools.partial(pack_kernel, whole=whole, listed=listed),
        out_shape=[near_shape] * (PLANE - 1) + [far_shape] * PLANE,
        grid_spec=pltpu.PrefetchScalarGridSpec(
            num_scalar_prefetch=2, grid=(), in_specs=[VMEM_SPEC] * len(whole), out_specs=[VMEM_SPEC] * (2 * PLANE - 1)
        ),
        compiler_params=PARAMS,
    )(plane, beyond, *held)
    return results[: PLANE - 1], results[PLANE - 1 :]


def gather_kernel(plane_ref, beyond_ref, *refs, whole, listed):
    near_parts, far_parts = refs[:PLANE], refs[PLANE : 2 * PLANE]
    targets = dict(zip(whole, refs[2 * PLANE :]))
    for target in targets.values():
        target[...] = jnp.zeros(target.shape, F32)

    def add(slot, target, source, place, rank):
        @pl.when(slot >= 0)
        def _():
            target[slot] = target[slot] + source[place, rank]

    for flip in range(PLANE):
        for rank in range(CAP):
            for place, offset in enumerate(whole):
                slot = plane_ref[(flip * len(whole) + place) * CAP + rank]
                add(slot, targets[offset], near_parts[flip], place, rank)
            for place, offset in enumerate(listed):
                slot = beyond_ref[(flip * len(listed) + place) * CAP + rank]
                add(slot, targets[offset ^ 1], far_parts[flip], place, rank)


def gather_sums(plane, beyond, near_parts, far_parts, whole, listed, blocks):
    rows, points = near_parts[0].shape[2:]
    operands = [*near_parts, *far_parts]
    return pl.pallas_call(
        functools.partial(gather_kernel, whole=whole, listed=listed),
        out_shape=[jax.ShapeDtypeStruct((blocks, rows, points), F32)] * len(whole),
        grid_spec=pltpu.PrefetchScalarGridSpec(
            num_scalar_prefetch=2, grid=(), in_specs=[VMEM_SPEC] * len(operands), out_specs=[VMEM_SPEC] * len(whole)
        ),
        compiler_params=PARAMS,
    )(plane, beyond, *operands)


def flip_move(array, bits):
    members = lax.axis_size("blk")
    return lax.ppermute(array, "blk", [(source, source ^ bits) for source in range(members)])


def local(probes, inverses, couplings, neighbour_devices, neighbour_slots):
    members = lax.axis_size("blk")
    position = lax.axis_index("blk")
    blocks = probes.shape[1]
    depth = members // PLANE
    whole, listed = line_offsets(depth)
    plane, beyond, fetch, put = tables(neighbour_devices, neighbour_slots, members, position)
    travel = sorted(whole[1:], key=lambda offset: (offset.bit_count(), -offset))

    def spread(panels, level):
        held = {0: panels}
        for offset in travel:
            bit = low_bit(offset)
            held[offset] = flip_move(held[offset ^ bit], bit * PLANE)
        held = [held[offset] for offset in whole]
        moved, far = pack(plane[level], beyond[level], held, whole, listed)
        moved = [flip_move(array, flip) for flip, array in enumerate(moved, 1)]
        far = [flip_move(array, PLANE | flip) for flip, array in enumerate(far)]
        return dict(held=held, moved=moved, far=far)

    def collect(near_parts, far_parts, level):
        near_parts = [near_parts[0]] + [flip_move(near_parts[flip], flip) for flip in range(1, PLANE)]
        far_parts = [flip_move(array, PLANE | flip) for flip, array in enumerate(far_parts)]
        sums = gather_sums(plane[level], beyond[level], near_parts, far_parts, whole, listed, blocks)
        sums = {offset: [array] for offset, array in zip(whole, sums)}
        for offset in travel[::-1]:
            bit = low_bit(offset)
            sums[offset ^ bit].append(flip_move(sum(sums[offset][1:], sums[offset][0]), bit * PLANE))
        return sums[0]

    chunks = range(CHUNKS)
    rows = probes.shape[2] // CHUNKS
    panels = [first(probes, inverses, chunk) for chunk in chunks]
    coupling = [halves(couplings, level, 4, 2) for level in range(LEVELS - 1)]
    inverse = [halves(inverses, level, 2, 1) for level in range(LEVELS)]
    call = functools.partial(solve, whole=whole, listed=listed)
    columns = []
    for chunk in chunks:
        forward = [panels[chunk]]
        solved = [None] * LEVELS
        for level in range(1, LEVELS):
            result, *parts = call(
                fetch[level - 1], put[level - 1], probes[level, :, chunk * rows : (chunk + 1) * rows],
                inverse[level], coupling[level - 1], **spread(forward[-1], level - 1), left=level == LEVELS - 1,
            )
            forward.append(result)
        solved[LEVELS - 1] = forward.pop()
        for level in range(LEVELS - 2, -1, -1):
            below = max(level - 1, 0)
            solved[level], *parts = call(
                fetch[below], put[below], forward[level], inverse[level], coupling[below] if level else None,
                sums=collect(*parts, level), left=True,
            )
        columns.append(jnp.stack(solved))
    return jnp.concatenate(columns, axis=2)


def solution(mesh):
    return jax.shard_map(
        local,
        mesh=mesh,
        in_specs=(
            P(None, ("grp", "blk"), None, None),
            P(None, ("grp", "blk"), None, None),
            P(None, ("grp", "blk"), None, None, None),
            P(None, "grp", None),
            P(None, "grp", None),
        ),
        out_specs=P(None, ("grp", "blk"), None, None),
        check_vma=False,
    )
```

```python
import functools

import jax
import jax.numpy as jnp
from jax import lax
from jax.experimental import pallas as pl
from jax.experimental.pallas import tpu as pltpu
from jax.sharding import PartitionSpec as P

LEVELS = 3
CAP = 2
CHUNKS = 2
CORE, SIDE, LINE = 1, 2, 4
F32 = jnp.float32
BF16 = jnp.bfloat16
NT = (((1,), (1,)), ((), ()))
NN = (((1,), (0,)), ((), ()))
PARAMS = pltpu.CompilerParams(vmem_limit_bytes=20 * 1024 * 1024)
VMEM_SPEC = pl.BlockSpec(memory_space=pltpu.VMEM)


def low_bit(offset):
    return offset & -offset


def in_hbm(array):
    return pltpu.with_memory_space_constraint(array, pltpu.HBM)


def in_vmem(array):
    return pltpu.with_memory_space_constraint(array, pltpu.VMEM)


def split(value):
    high = value.astype(BF16)
    return high, (value - high.astype(F32)).astype(BF16)


def product(panel, high, low, dims):
    rows = panel.shape[0]
    panel_high, panel_low = split(panel)
    both = lax.dot_general(
        jnp.concatenate([panel_high, panel_low], axis=0), high, dims, preferred_element_type=F32
    )
    cross = lax.dot_general(panel_high, low, dims, preferred_element_type=F32)
    return both[:rows] + (both[rows:] + cross)


def line_offsets(depth):
    whole = tuple(offset for offset in range(depth) if offset % 2 == 0 or offset == 1)
    return whole, tuple(offset for offset in range(depth) if offset not in whole)


def lookup(values, index):
    hits = index[..., None] == jnp.arange(len(values))
    return jnp.sum(jnp.where(hits, jnp.array(values, jnp.int32), 0), axis=-1)


def tables(dev_rows, slot_rows, members, position):
    levels, rows, fanout = dev_rows.shape
    blocks_dev = rows // members
    width = blocks_dev * fanout
    depth = members // LINE
    whole, listed = line_offsets(depth)
    height, place = position // LINE, position % LINE

    readers = jnp.stack([position, position ^ SIDE, position ^ LINE, position ^ (LINE | SIDE)])
    lists = jnp.take(dev_rows.reshape(levels, members, width), readers, axis=1)
    slots = jnp.take(slot_rows.reshape(levels, members, width), readers, axis=1)
    positions = jnp.arange(width)
    earlier = positions[None, :] < positions[:, None]
    matches = lists[..., :, None] == lists[..., None, :]
    rank = jnp.sum(jnp.logical_and(matches, earlier), axis=-1, dtype=jnp.int32)
    code = lists * CAP + rank

    def asked(reader, offsets):
        owners = (height ^ jnp.array(offsets, jnp.int32))[:, None] * LINE + (place ^ jnp.arange(2))[None, :]
        wanted = (owners[..., None] * CAP + jnp.arange(CAP)).reshape(-1)
        found = code[:, reader, None, :] == wanted[None, :, None]
        return jnp.sum(jnp.where(found, slots[:, reader, None, :] + 1, 0), axis=2) - 1

    across = tuple(offset ^ 1 for offset in listed)
    table = jnp.concatenate([asked(1, whole), asked(2, across), asked(3, across)], axis=1)
    own_dev, own_slot, own_rank = lists[:, 0], slots[:, 0], rank[:, 0]
    flip = (own_dev % LINE) ^ place
    side, core = flip // SIDE, flip % SIDE
    offset = (own_dev // LINE) ^ height
    spot = lookup([whole.index(o) if o in whole else listed.index(o) for o in range(depth)], offset)
    is_whole = lookup([int(o in whole) for o in range(depth)], offset) == 1
    at_side = len(whole) * 2 * blocks_dev
    at_far = at_side + len(whole) * 2 * CAP
    place_of = jnp.where(
        is_whole,
        jnp.where(
            side == 0,
            (spot * 2 + core) * blocks_dev + own_slot,
            at_side + (spot * 2 + core) * CAP + own_rank,
        ),
        at_far + ((side * len(listed) + spot) * 2 + core) * CAP + own_rank,
    )
    return table.reshape(-1), place_of.reshape(-1)


COST = pl.CostEstimate(flops=600_000_000, bytes_accessed=3_000_000, transcendentals=0)


def run(kernel, out_shape, tables, operands, specs=None, scratch=(), grid=(), out_specs=None):
    return pl.pallas_call(
        kernel,
        out_shape=out_shape,
        grid_spec=pltpu.PrefetchScalarGridSpec(
            num_scalar_prefetch=len(tables),
            grid=grid,
            in_specs=specs if specs is not None else [VMEM_SPEC] * len(operands),
            out_specs=out_specs if out_specs is not None else [VMEM_SPEC] * len(out_shape),
            scratch_shapes=list(scratch),
        ),
        compiler_params=PARAMS,
        cost_estimate=COST,
    )(*tables, *operands)


def halves_kernel(*refs, streams, count):
    step = pl.program_id(0)
    for stream in range(streams):
        high, low = split(refs[stream][...])
        at = pl.ds((stream * count + step) * high.shape[0], high.shape[0])
        refs[streams][at], refs[streams + 1][at] = high, low


def halves(matrices, level, streams, width):
    points = matrices.shape[-1]
    matrices = matrices.reshape(matrices.shape[0], -1, points, points)
    total = matrices.shape[1]
    count = total // (streams * width)
    shape = pltpu.VMEM((total, points, points), BF16)
    specs = [
        pl.BlockSpec((None, width, points, points), lambda step, stream=stream: (level, stream * count + step, 0, 0))
        for stream in range(streams)
    ]
    return run(
        functools.partial(halves_kernel, streams=streams, count=count),
        [shape, shape], (), [in_hbm(matrices)] * streams, specs, grid=(count,),
    )


def first_kernel(probe_ref, inverse_ref, forward_ref):
    for g in range(inverse_ref.shape[0]):
        forward_ref[g] = product(probe_ref[g], *split(inverse_ref[g]), NT)


def first(probes, inverses, chunk):
    blocks, rows, points = probes.shape[1], probes.shape[2] // CHUNKS, probes.shape[3]
    width = blocks // 2 if blocks % 2 == 0 else blocks
    return run(
        first_kernel,
        [jax.ShapeDtypeStruct((blocks, rows, points), F32)],
        (), [in_hbm(probes), in_hbm(inverses)],
        [
            pl.BlockSpec((None, width, rows, points), lambda g: (0, g, chunk, 0)),
            pl.BlockSpec((None, width, points, points), lambda g: (0, g, 0, 0)),
        ],
        grid=(blocks // width,),
        out_specs=[pl.BlockSpec((width, rows, points), lambda g: (g, 0, 0))],
    )[0]


def pack_kernel(asked_ref, *refs, base, whole, listed):
    sources, targets = refs[: 2 * len(whole)], refs[2 * len(whole) :]
    row = 0
    for target, offsets in zip(targets, (whole, listed, listed)):
        for place, offset in enumerate(offsets):
            held = whole.index(offset if offsets is whole else offset ^ 1)
            for core in range(2):
                for rank in range(CAP):
                    slot = jnp.maximum(asked_ref[base + row * CAP + rank], 0)
                    target[(place * 2 + core) * CAP + rank] = sources[held * 2 + core][slot]
                row += 1


def pack(asked, base, held, whole, listed):
    rows, points = held[0].shape[1:]
    return run(
        functools.partial(pack_kernel, base=base, whole=whole, listed=listed),
        [
            jax.ShapeDtypeStruct((len(offsets) * 2 * CAP, rows, points), F32)
            for offsets in (whole, listed, listed)
        ],
        (asked,), held,
    )


def gather_kernel(asked_ref, local_ref, *refs, base, whole, listed, blocks):
    sources, (keep_ref, give_ref) = refs[:3], refs[3:]
    for place in range(len(whole)):
        for core, target in enumerate((keep_ref, give_ref)):
            target[place] = local_ref[pl.ds((place * 2 + core) * blocks, blocks)]
    row = 0
    for source, offsets in zip(sources, (whole, listed, listed)):
        for place, offset in enumerate(offsets):
            held = whole.index(offset if offsets is whole else offset ^ 1)
            for core, target in enumerate((keep_ref, give_ref)):
                for rank in range(CAP):
                    slot = asked_ref[base + row * CAP + rank]
                    term = source[(place * 2 + core) * CAP + rank]

                    @pl.when(slot >= 0)
                    def _(target=target, held=held, slot=slot, term=term):
                        target[held, slot] = target[held, slot] + term

                row += 1


def gather_sums(asked, base, local, moved, whole, listed, blocks):
    rows, points = local.shape[1:]
    shape = jax.ShapeDtypeStruct((len(whole), blocks, rows, points), F32)
    return run(
        functools.partial(gather_kernel, base=base, whole=whole, listed=listed, blocks=blocks),
        [shape, shape], (asked,), [local, *moved],
    )


def add_kernel(first_ref, second_ref, *targets):
    for place, target in enumerate(targets, 1):
        target[...] = first_ref[place] + second_ref[place]


def add(kept, given):
    shape = jax.ShapeDtypeStruct(kept.shape[1:], F32)
    return run(add_kernel, [shape] * (kept.shape[0] - 1), (), [kept, given])


def solve_kernel(
    place_ref, panel_ref, *refs, has_fetch, has_left, has_parts, base, level, chunk, whole, listed, blocks, fanout, adds
):
    refs = list(refs)

    def take(count):
        taken, refs[:count] = refs[:count], []
        return taken

    inverse_refs = take(2)
    coupling_refs = take(2) if has_fetch or has_parts else None
    near_refs = take(2 * len(whole)) if has_fetch else []
    far_refs = take(3) if has_fetch else []
    sum_refs = take(2 + adds) if not has_fetch else []
    (out_ref,) = take(1)
    part_refs = take(4) if has_parts else []
    pan_ref = take(1)[0] if has_fetch else None
    hold_ref = take(1)[0] if has_parts else None
    rows = out_ref.shape[1]
    start = 0
    for ref in near_refs + far_refs:
        pan_ref[pl.ds(start, ref.shape[0])] = ref[...]
        start += ref.shape[0]
    if has_parts:
        hold_ref[...] = jnp.zeros(hold_ref.shape, F32)
    for g in range(blocks):
        inverse = [ref[level * blocks + g] for ref in inverse_refs]
        if has_fetch:
            value = panel_ref[level, g, pl.ds(chunk * rows, rows)]
            for k in range(fanout):
                coupling = [ref[g * fanout + k] for ref in coupling_refs]
                value = value - product(pan_ref[place_ref[base + g * fanout + k]], *coupling, NT)
            value = product(value, *inverse, NT)
        else:
            value = panel_ref[g] - sum_refs[0][0, g] - sum_refs[1][0, g]
            for ref in sum_refs[2:]:
                value = value - ref[g]
        if has_left:
            value = product(value, *inverse, NN)
        out_ref[g] = value
        if has_parts:
            for k in range(fanout):
                coupling = [ref[g * fanout + k] for ref in coupling_refs]
                at = place_ref[base + g * fanout + k]
                hold_ref[at] = hold_ref[at] + product(value, *coupling, NN)
    start = 0
    for ref in part_refs:
        ref[...] = hold_ref[pl.ds(start, ref.shape[0])]
        start += ref.shape[0]


def solve(
    places, base, panel, rows, level, chunk, inverse, coupling, whole, listed, blocks,
    near=None, far=None, sums=None, left=False,
):
    points = panel.shape[-1]
    has_fetch = near is not None
    has_parts = left and coupling is not None
    fanout = coupling[0].shape[0] // blocks if coupling is not None else 0
    operands = [panel, *[in_vmem(array) for array in [*inverse, *(coupling if coupling is not None else [])]]]
    operands += [*near, *far] if has_fetch else sums
    out_shapes = [jax.ShapeDtypeStruct((blocks, rows, points), F32)]
    sizes = [len(whole) * 2 * blocks, len(whole) * 2 * CAP, len(listed) * 2 * CAP, len(listed) * 2 * CAP]
    scratch = [pltpu.VMEM((sum(sizes), rows, points), F32)] * (has_fetch + has_parts)
    if has_parts:
        out_shapes += [jax.ShapeDtypeStruct((size, rows, points), F32) for size in sizes]
    kernel = functools.partial(
        solve_kernel, has_fetch=has_fetch, has_left=left, has_parts=has_parts, base=base, level=level, chunk=chunk,
        whole=whole, listed=listed, blocks=blocks, fanout=fanout, adds=0 if has_fetch else len(sums) - 2,
    )
    results = run(kernel, out_shapes, (places,), operands, scratch=scratch)
    return results[0], results[1:]


def flip_move(array, bits):
    members = lax.axis_size("blk")
    return lax.ppermute(array, "blk", [(source, source ^ bits) for source in range(members)])


def local(probes, inverses, couplings, neighbour_devices, neighbour_slots):
    members = lax.axis_size("blk")
    position = lax.axis_index("blk")
    blocks, fanout = probes.shape[1], couplings.shape[2]
    rows = probes.shape[2] // CHUNKS
    depth = members // LINE
    whole, listed = line_offsets(depth)
    asked, places = tables(neighbour_devices, neighbour_slots, members, position)
    asked_size, place_size = asked.shape[0] // (LEVELS - 1), places.shape[0] // (LEVELS - 1)
    travel = sorted(whole[1:], key=lambda offset: (offset.bit_count(), -offset))
    shared = {}
    columns = [None] * CHUNKS

    def chain(chunk):
        call = functools.partial(
            solve, places, rows=rows, chunk=chunk, whole=whole, listed=listed, blocks=blocks
        )
        forward = [first(probes, inverses, chunk)]
        solved = [None] * LEVELS
        parts = None
        for level in range(1, LEVELS):
            held = {0: forward[-1]}
            for offset in travel:
                bit = low_bit(offset)
                held[offset] = flip_move(held[offset ^ bit], bit * LINE)
            near = [array for offset in whole for array in (held[offset], flip_move(held[offset], CORE))]
            yield
            packs = pack(asked, (level - 1) * asked_size, near, whole, listed)
            far = [flip_move(array, bits) for array, bits in zip(packs, (SIDE, LINE, LINE | SIDE))]
            yield
            result, parts = call(
                base=(level - 1) * place_size, panel=shared["probes"], level=level, inverse=shared["inverse"],
                coupling=shared["coupling"][level - 1], near=near, far=far, left=level == LEVELS - 1,
            )
            forward.append(result)
        solved[LEVELS - 1] = forward.pop()
        for level in range(LEVELS - 2, -1, -1):
            moved = [flip_move(array, bits) for array, bits in zip(parts[1:], (SIDE, LINE, LINE | SIDE))]
            yield
            kept, gift = gather_sums(asked, level * asked_size, parts[0], moved, whole, listed, blocks)
            given = flip_move(gift, CORE)
            yield
            totals = dict(zip(whole[1:], add(kept, given)))
            addends = []
            for offset in travel[::-1]:
                bit = low_bit(offset)
                arrived = flip_move(totals[offset], bit * LINE)
                if offset == bit:
                    addends.append(arrived)
                else:
                    totals[offset ^ bit] = totals[offset ^ bit] + arrived
            yield
            solved[level], parts = call(
                base=max(level - 1, 0) * place_size, panel=forward[level], level=level, inverse=shared["inverse"],
                coupling=shared["coupling"][level - 1] if level else None, sums=[kept, given, *addends], left=True,
            )
        columns[chunk] = jnp.stack(solved)
        yield

    def prepare_couplings(level):
        shared.setdefault("coupling", {})[level] = halves(couplings, level, 4, max(1, blocks * fanout // 12))

    def prepare_inverses():
        every = inverses.reshape(1, -1, *inverses.shape[2:])
        shared["inverse"] = halves(every, 0, 3, blocks // 2 if blocks % 2 == 0 else blocks)
        shared["probes"] = probes

    chains = [chain(chunk) for chunk in range(CHUNKS)]
    for stage in range(4 * LEVELS):
        if stage == 1:
            prepare_inverses()
            for level in range(LEVELS - 1):
                prepare_couplings(level)
        for steps in chains:
            next(steps, None)
    return jnp.concatenate(columns, axis=2)


def solution(mesh):
    return jax.shard_map(
        local,
        mesh=mesh,
        in_specs=(
            P(None, ("grp", "blk"), None, None),
            P(None, ("grp", "blk"), None, None),
            P(None, ("grp", "blk"), None, None, None),
            P(None, "grp", None),
            P(None, "grp", None),
        ),
        out_specs=P(None, ("grp", "blk"), None, None),
        check_vma=False,
    )
```

```python
import functools

import jax
import jax.numpy as jnp
from jax import lax
from jax.experimental import pallas as pl
from jax.experimental.pallas import tpu as pltpu
from jax.sharding import PartitionSpec as P

LEVELS = 3
CAP = 2
CHUNKS = 2
STAGGERED = (1,)
CORE, SIDE, LINE = 1, 2, 4
F32 = jnp.float32
BF16 = jnp.bfloat16
NT = (((1,), (1,)), ((), ()))
NN = (((1,), (0,)), ((), ()))
PARAMS = pltpu.CompilerParams(vmem_limit_bytes=20 * 1024 * 1024)
VMEM_SPEC = pl.BlockSpec(memory_space=pltpu.VMEM)


def low_bit(offset):
    return offset & -offset


def in_hbm(array):
    return pltpu.with_memory_space_constraint(array, pltpu.HBM)


def in_vmem(array):
    return pltpu.with_memory_space_constraint(array, pltpu.VMEM)


def split(value):
    high = value.astype(BF16)
    return high, (value - high.astype(F32)).astype(BF16)


def product(panel, high, low, dims):
    rows = panel.shape[0]
    panel_high, panel_low = split(panel)
    both = lax.dot_general(
        jnp.concatenate([panel_high, panel_low], axis=0), high, dims, preferred_element_type=F32
    )
    cross = lax.dot_general(panel_high, low, dims, preferred_element_type=F32)
    return both[:rows] + (both[rows:] + cross)


def line_offsets(depth):
    whole = tuple(offset for offset in range(depth) if offset % 2 == 0 or offset == 1)
    return whole, tuple(offset for offset in range(depth) if offset not in whole)


def lookup(values, index):
    hits = index[..., None] == jnp.arange(len(values))
    return jnp.sum(jnp.where(hits, jnp.array(values, jnp.int32), 0), axis=-1)


def tables(dev_rows, slot_rows, members, position):
    levels, rows, fanout = dev_rows.shape
    blocks_dev = rows // members
    width = blocks_dev * fanout
    depth = members // LINE
    whole, listed = line_offsets(depth)
    height, place = position // LINE, position % LINE

    readers = jnp.stack([position, position ^ SIDE, position ^ LINE, position ^ (LINE | SIDE)])
    lists = jnp.take(dev_rows.reshape(levels, members, width), readers, axis=1)
    slots = jnp.take(slot_rows.reshape(levels, members, width), readers, axis=1)
    positions = jnp.arange(width)
    earlier = positions[None, :] < positions[:, None]
    matches = lists[..., :, None] == lists[..., None, :]
    rank = jnp.sum(jnp.logical_and(matches, earlier), axis=-1, dtype=jnp.int32)
    code = lists * CAP + rank

    def asked(reader, offsets):
        owners = (height ^ jnp.array(offsets, jnp.int32))[:, None] * LINE + (place ^ jnp.arange(2))[None, :]
        wanted = (owners[..., None] * CAP + jnp.arange(CAP)).reshape(-1)
        found = code[:, reader, None, :] == wanted[None, :, None]
        return jnp.sum(jnp.where(found, slots[:, reader, None, :] + 1, 0), axis=2) - 1

    across = tuple(offset ^ 1 for offset in listed)
    table = jnp.concatenate([asked(1, whole), asked(2, across), asked(3, across)], axis=1)
    own_dev, own_slot, own_rank = lists[:, 0], slots[:, 0], rank[:, 0]
    flip = (own_dev % LINE) ^ place
    side, core = flip // SIDE, flip % SIDE
    offset = (own_dev // LINE) ^ height
    spot = lookup([whole.index(o) if o in whole else listed.index(o) for o in range(depth)], offset)
    is_whole = lookup([int(o in whole) for o in range(depth)], offset) == 1
    at_side = len(whole) * 2 * blocks_dev
    at_far = at_side + len(whole) * 2 * CAP
    place_of = jnp.where(
        is_whole,
        jnp.where(
            side == 0,
            (spot * 2 + core) * blocks_dev + own_slot,
            at_side + (spot * 2 + core) * CAP + own_rank,
        ),
        at_far + ((side * len(listed) + spot) * 2 + core) * CAP + own_rank,
    )
    return table.reshape(-1), place_of.reshape(-1)


COST = pl.CostEstimate(flops=600_000_000, bytes_accessed=3_000_000, transcendentals=0)


def run(kernel, out_shape, tables, operands, specs=None, scratch=(), grid=(), out_specs=None):
    return pl.pallas_call(
        kernel,
        out_shape=out_shape,
        grid_spec=pltpu.PrefetchScalarGridSpec(
            num_scalar_prefetch=len(tables),
            grid=grid,
            in_specs=specs if specs is not None else [VMEM_SPEC] * len(operands),
            out_specs=out_specs if out_specs is not None else [VMEM_SPEC] * len(out_shape),
            scratch_shapes=list(scratch),
        ),
        compiler_params=PARAMS,
        cost_estimate=COST,
    )(*tables, *operands)


def halves_kernel(*refs, streams, count):
    step = pl.program_id(0)
    for stream in range(streams):
        high, low = split(refs[stream][...])
        at = pl.ds((stream * count + step) * high.shape[0], high.shape[0])
        refs[streams][at], refs[streams + 1][at] = high, low


def halves(matrices, level, streams, width):
    points = matrices.shape[-1]
    matrices = matrices.reshape(matrices.shape[0], -1, points, points)
    total = matrices.shape[1]
    count = total // (streams * width)
    shape = pltpu.VMEM((total, points, points), BF16)
    specs = [
        pl.BlockSpec((None, width, points, points), lambda step, stream=stream: (level, stream * count + step, 0, 0))
        for stream in range(streams)
    ]
    return run(
        functools.partial(halves_kernel, streams=streams, count=count),
        [shape, shape], (), [in_hbm(matrices)] * streams, specs, grid=(count,),
    )


def first_kernel(probe_ref, inverse_ref, forward_ref):
    for g in range(inverse_ref.shape[0]):
        forward_ref[g] = product(probe_ref[g], *split(inverse_ref[g]), NT)


def first(probes, inverses, chunk):
    blocks, rows, points = probes.shape[1], probes.shape[2] // CHUNKS, probes.shape[3]
    width = blocks // 2 if blocks % 2 == 0 else blocks
    return run(
        first_kernel,
        [jax.ShapeDtypeStruct((blocks, rows, points), F32)],
        (), [in_hbm(probes), in_hbm(inverses)],
        [
            pl.BlockSpec((None, width, rows, points), lambda g: (0, g, chunk, 0)),
            pl.BlockSpec((None, width, points, points), lambda g: (0, g, 0, 0)),
        ],
        grid=(blocks // width,),
        out_specs=[pl.BlockSpec((width, rows, points), lambda g: (g, 0, 0))],
    )[0]


def pack_kernel(asked_ref, *refs, base, whole, listed):
    sources, targets = refs[: 2 * len(whole)], refs[2 * len(whole) :]
    row = 0
    for target, offsets in zip(targets, (whole, listed, listed)):
        for place, offset in enumerate(offsets):
            held = whole.index(offset if offsets is whole else offset ^ 1)
            for core in range(2):
                for rank in range(CAP):
                    slot = jnp.maximum(asked_ref[base + row * CAP + rank], 0)
                    target[(place * 2 + core) * CAP + rank] = sources[held * 2 + core][slot]
                row += 1


def pack(asked, base, held, whole, listed):
    rows, points = held[0].shape[1:]
    return run(
        functools.partial(pack_kernel, base=base, whole=whole, listed=listed),
        [
            jax.ShapeDtypeStruct((len(offsets) * 2 * CAP, rows, points), F32)
            for offsets in (whole, listed, listed)
        ],
        (asked,), held,
    )


def gather_kernel(asked_ref, local_ref, *refs, base, whole, listed, blocks):
    sources, (keep_ref, give_ref) = refs[:3], refs[3:]
    for place in range(len(whole)):
        for core, target in enumerate((keep_ref, give_ref)):
            target[place] = local_ref[pl.ds((place * 2 + core) * blocks, blocks)]
    row = 0
    for source, offsets in zip(sources, (whole, listed, listed)):
        for place, offset in enumerate(offsets):
            held = whole.index(offset if offsets is whole else offset ^ 1)
            for core, target in enumerate((keep_ref, give_ref)):
                for rank in range(CAP):
                    slot = asked_ref[base + row * CAP + rank]
                    term = source[(place * 2 + core) * CAP + rank]

                    @pl.when(slot >= 0)
                    def _(target=target, held=held, slot=slot, term=term):
                        target[held, slot] = target[held, slot] + term

                row += 1


def gather_sums(asked, base, local, moved, whole, listed, blocks):
    rows, points = local.shape[1:]
    shape = jax.ShapeDtypeStruct((len(whole), blocks, rows, points), F32)
    return run(
        functools.partial(gather_kernel, base=base, whole=whole, listed=listed, blocks=blocks),
        [shape, shape], (asked,), [local, *moved],
    )


def add_kernel(first_ref, second_ref, *targets):
    for place, target in enumerate(targets, 1):
        target[...] = first_ref[place] + second_ref[place]


def add(kept, given):
    shape = jax.ShapeDtypeStruct(kept.shape[1:], F32)
    return run(add_kernel, [shape] * (kept.shape[0] - 1), (), [kept, given])


def solve_kernel(
    place_ref, panel_ref, *refs, has_fetch, has_left, has_parts, base, level, chunk, whole, listed, blocks, fanout, adds
):
    refs = list(refs)

    def take(count):
        taken, refs[:count] = refs[:count], []
        return taken

    inverse_refs = take(2)
    coupling_refs = take(2) if has_fetch or has_parts else None
    near_refs = take(2 * len(whole)) if has_fetch else []
    far_refs = take(3) if has_fetch else []
    sum_refs = take(2 + adds) if not has_fetch else []
    (out_ref,) = take(1)
    part_refs = take(4) if has_parts else []
    pan_ref = take(1)[0] if has_fetch else None
    hold_ref = take(1)[0] if has_parts else None
    rows = out_ref.shape[1]
    start = 0
    for ref in near_refs + far_refs:
        pan_ref[pl.ds(start, ref.shape[0])] = ref[...]
        start += ref.shape[0]
    if has_parts:
        hold_ref[...] = jnp.zeros(hold_ref.shape, F32)
    for g in range(blocks):
        inverse = [ref[level * blocks + g] for ref in inverse_refs]
        if has_fetch:
            value = panel_ref[level, g, pl.ds(chunk * rows, rows)]
            for k in range(fanout):
                coupling = [ref[g * fanout + k] for ref in coupling_refs]
                value = value - product(pan_ref[place_ref[base + g * fanout + k]], *coupling, NT)
            value = product(value, *inverse, NT)
        else:
            value = panel_ref[g] - sum_refs[0][0, g] - sum_refs[1][0, g]
            for ref in sum_refs[2:]:
                value = value - ref[g]
        if has_left:
            value = product(value, *inverse, NN)
        out_ref[g] = value
        if has_parts:
            for k in range(fanout):
                coupling = [ref[g * fanout + k] for ref in coupling_refs]
                at = place_ref[base + g * fanout + k]
                hold_ref[at] = hold_ref[at] + product(value, *coupling, NN)
    start = 0
    for ref in part_refs:
        ref[...] = hold_ref[pl.ds(start, ref.shape[0])]
        start += ref.shape[0]


def solve(
    places, base, panel, rows, level, chunk, inverse, coupling, whole, listed, blocks,
    near=None, far=None, sums=None, left=False,
):
    points = panel.shape[-1]
    has_fetch = near is not None
    has_parts = left and coupling is not None
    fanout = coupling[0].shape[0] // blocks if coupling is not None else 0
    operands = [panel, *[in_vmem(array) for array in [*inverse, *(coupling if coupling is not None else [])]]]
    operands += [*near, *far] if has_fetch else sums
    out_shapes = [jax.ShapeDtypeStruct((blocks, rows, points), F32)]
    sizes = [len(whole) * 2 * blocks, len(whole) * 2 * CAP, len(listed) * 2 * CAP, len(listed) * 2 * CAP]
    scratch = [pltpu.VMEM((sum(sizes), rows, points), F32)] * (has_fetch + has_parts)
    if has_parts:
        out_shapes += [jax.ShapeDtypeStruct((size, rows, points), F32) for size in sizes]
    kernel = functools.partial(
        solve_kernel, has_fetch=has_fetch, has_left=left, has_parts=has_parts, base=base, level=level, chunk=chunk,
        whole=whole, listed=listed, blocks=blocks, fanout=fanout, adds=0 if has_fetch else len(sums) - 2,
    )
    results = run(kernel, out_shapes, (places,), operands, scratch=scratch)
    return results[0], results[1:]


def flip_move(array, bits):
    members = lax.axis_size("blk")
    return lax.ppermute(array, "blk", [(source, source ^ bits) for source in range(members)])


def local(probes, inverses, couplings, neighbour_devices, neighbour_slots):
    members = lax.axis_size("blk")
    position = lax.axis_index("blk")
    blocks, fanout = probes.shape[1], couplings.shape[2]
    rows = probes.shape[2] // CHUNKS
    depth = members // LINE
    whole, listed = line_offsets(depth)
    asked, places = tables(neighbour_devices, neighbour_slots, members, position)
    asked_size, place_size = asked.shape[0] // (LEVELS - 1), places.shape[0] // (LEVELS - 1)
    travel = sorted(whole[1:], key=lambda offset: (offset.bit_count(), -offset))
    shared, ahead = {}, {}
    columns = [None] * CHUNKS

    def chain(chunk):
        call = functools.partial(
            solve, places, rows=rows, chunk=chunk, whole=whole, listed=listed, blocks=blocks
        )
        forward = [first(probes, inverses, chunk)]
        solved = [None] * LEVELS
        parts = None
        for level in range(1, LEVELS):
            held = {0: forward[-1]}
            for offset in travel:
                bit = low_bit(offset)
                held[offset] = flip_move(held[offset ^ bit], bit * LINE)
            near = []
            for offset in whole:
                swapped = held[offset]
                if offset and (level, chunk - 1) in ahead:
                    swapped, _ = lax.optimization_barrier((swapped, ahead[level, chunk - 1]))
                near += [held[offset], flip_move(swapped, CORE)]
            packs = pack(asked, (level - 1) * asked_size, near, whole, listed)
            if level in STAGGERED:
                ahead[level, chunk] = packs[0]
            far = [flip_move(array, bits) for array, bits in zip(packs, (SIDE, LINE, LINE | SIDE))]
            yield
            result, parts = call(
                base=(level - 1) * place_size, panel=shared["probes"], level=level, inverse=shared["inverse"],
                coupling=shared["coupling"][level - 1], near=near, far=far, left=level == LEVELS - 1,
            )
            forward.append(result)
        solved[LEVELS - 1] = forward.pop()
        for level in range(LEVELS - 2, -1, -1):
            moved = [flip_move(array, bits) for array, bits in zip(parts[1:], (SIDE, LINE, LINE | SIDE))]
            yield
            kept, gift = gather_sums(asked, level * asked_size, parts[0], moved, whole, listed, blocks)
            given = flip_move(gift, CORE)
            yield
            totals = dict(zip(whole[1:], add(kept, given)))
            addends = []
            for offset in travel[::-1]:
                bit = low_bit(offset)
                arrived = flip_move(totals[offset], bit * LINE)
                if offset == bit:
                    addends.append(arrived)
                else:
                    totals[offset ^ bit] = totals[offset ^ bit] + arrived
            yield
            solved[level], parts = call(
                base=max(level - 1, 0) * place_size, panel=forward[level], level=level, inverse=shared["inverse"],
                coupling=shared["coupling"][level - 1] if level else None, sums=[kept, given, *addends], left=True,
            )
        columns[chunk] = jnp.stack(solved)
        yield

    def prepare_couplings(level):
        shared.setdefault("coupling", {})[level] = halves(couplings, level, 4, max(1, blocks * fanout // 12))

    def prepare_inverses():
        every = inverses.reshape(1, -1, *inverses.shape[2:])
        shared["inverse"] = halves(every, 0, 3, blocks // 2 if blocks % 2 == 0 else blocks)
        shared["probes"] = probes

    chains = [chain(chunk) for chunk in range(CHUNKS)]
    for stage in range(4 * LEVELS):
        if stage == 1:
            prepare_inverses()
            for level in range(LEVELS - 1):
                prepare_couplings(level)
        for steps in chains:
            next(steps, None)
    return jnp.concatenate(columns, axis=2)


def solution(mesh):
    return jax.shard_map(
        local,
        mesh=mesh,
        in_specs=(
            P(None, ("grp", "blk"), None, None),
            P(None, ("grp", "blk"), None, None),
            P(None, ("grp", "blk"), None, None, None),
            P(None, "grp", None),
            P(None, "grp", None),
        ),
        out_specs=P(None, ("grp", "blk"), None, None),
        check_vma=False,
    )
```

```python
import functools

import jax
import jax.numpy as jnp
from jax import lax
from jax.experimental import pallas as pl
from jax.experimental.pallas import tpu as pltpu
from jax.sharding import PartitionSpec as P

LEVELS = 3
CAP = 2
CHUNKS = 2
STAGGERED = (1,)
CORE, SIDE, LINE = 1, 2, 4
F32 = jnp.float32
BF16 = jnp.bfloat16
NT = (((1,), (1,)), ((), ()))
NN = (((1,), (0,)), ((), ()))
PARAMS = pltpu.CompilerParams(vmem_limit_bytes=20 * 1024 * 1024)
VMEM_SPEC = pl.BlockSpec(memory_space=pltpu.VMEM)
ANY_SPEC = pl.BlockSpec(memory_space=pl.ANY)


def low_bit(offset):
    return offset & -offset


def in_hbm(array):
    return pltpu.with_memory_space_constraint(array, pltpu.HBM)


def in_vmem(array):
    return pltpu.with_memory_space_constraint(array, pltpu.VMEM)


def split(value):
    high = value.astype(BF16)
    return high, (value - high.astype(F32)).astype(BF16)


def product(panel, high, low, dims):
    rows = panel.shape[0]
    panel_high, panel_low = split(panel)
    both = lax.dot_general(
        jnp.concatenate([panel_high, panel_low], axis=0), high, dims, preferred_element_type=F32
    )
    cross = lax.dot_general(panel_high, low, dims, preferred_element_type=F32)
    return both[:rows] + (both[rows:] + cross)


def line_offsets(depth):
    whole = tuple(offset for offset in range(depth) if offset % 2 == 0 or offset == 1)
    return whole, tuple(offset for offset in range(depth) if offset not in whole)


def lookup(values, index):
    hits = index[..., None] == jnp.arange(len(values))
    return jnp.sum(jnp.where(hits, jnp.array(values, jnp.int32), 0), axis=-1)


def tables(dev_rows, slot_rows, members, position):
    levels, rows, fanout = dev_rows.shape
    blocks_dev = rows // members
    width = blocks_dev * fanout
    depth = members // LINE
    whole, listed = line_offsets(depth)
    height, place = position // LINE, position % LINE

    readers = jnp.stack([position, position ^ SIDE, position ^ LINE, position ^ (LINE | SIDE)])
    lists = jnp.take(dev_rows.reshape(levels, members, width), readers, axis=1)
    slots = jnp.take(slot_rows.reshape(levels, members, width), readers, axis=1)
    positions = jnp.arange(width)
    earlier = positions[None, :] < positions[:, None]
    matches = lists[..., :, None] == lists[..., None, :]
    rank = jnp.sum(jnp.logical_and(matches, earlier), axis=-1, dtype=jnp.int32)
    code = lists * CAP + rank

    def asked(reader, offsets):
        owners = (height ^ jnp.array(offsets, jnp.int32))[:, None] * LINE + (place ^ jnp.arange(2))[None, :]
        wanted = (owners[..., None] * CAP + jnp.arange(CAP)).reshape(-1)
        found = code[:, reader, None, :] == wanted[None, :, None]
        return jnp.sum(jnp.where(found, slots[:, reader, None, :] + 1, 0), axis=2) - 1

    across = tuple(offset ^ 1 for offset in listed)
    table = jnp.concatenate([asked(1, whole), asked(2, across), asked(3, across)], axis=1)
    own_dev, own_slot, own_rank = lists[:, 0], slots[:, 0], rank[:, 0]
    flip = (own_dev % LINE) ^ place
    side, core = flip // SIDE, flip % SIDE
    offset = (own_dev // LINE) ^ height
    spot = lookup([whole.index(o) if o in whole else listed.index(o) for o in range(depth)], offset)
    is_whole = lookup([int(o in whole) for o in range(depth)], offset) == 1
    at_side = len(whole) * 2 * blocks_dev
    at_far = at_side + len(whole) * 2 * CAP
    place_of = jnp.where(
        is_whole,
        jnp.where(
            side == 0,
            (spot * 2 + core) * blocks_dev + own_slot,
            at_side + (spot * 2 + core) * CAP + own_rank,
        ),
        at_far + ((side * len(listed) + spot) * 2 + core) * CAP + own_rank,
    )
    return table.reshape(-1), place_of.reshape(-1)


COST = pl.CostEstimate(flops=600_000_000, bytes_accessed=3_000_000, transcendentals=0)


def run(kernel, out_shape, tables, operands, specs=None, scratch=(), grid=(), out_specs=None):
    return pl.pallas_call(
        kernel,
        out_shape=out_shape,
        grid_spec=pltpu.PrefetchScalarGridSpec(
            num_scalar_prefetch=len(tables),
            grid=grid,
            in_specs=specs if specs is not None else [VMEM_SPEC] * len(operands),
            out_specs=out_specs if out_specs is not None else [VMEM_SPEC] * len(out_shape),
            scratch_shapes=list(scratch),
        ),
        compiler_params=PARAMS,
        cost_estimate=COST,
    )(*tables, *operands)


def halves_kernel(*refs, streams, count):
    step = pl.program_id(0)
    for stream in range(streams):
        high, low = split(refs[stream][...])
        at = pl.ds((stream * count + step) * high.shape[0], high.shape[0])
        refs[streams][at], refs[streams + 1][at] = high, low


def halves(matrices, level, streams, width):
    points = matrices.shape[-1]
    matrices = matrices.reshape(matrices.shape[0], -1, points, points)
    total = matrices.shape[1]
    count = total // (streams * width)
    shape = pltpu.VMEM((total, points, points), BF16)
    specs = [
        pl.BlockSpec((None, width, points, points), lambda step, stream=stream: (level, stream * count + step, 0, 0))
        for stream in range(streams)
    ]
    return run(
        functools.partial(halves_kernel, streams=streams, count=count),
        [shape, shape], (), [in_hbm(matrices)] * streams, specs, grid=(count,),
    )


def first_kernel(probe_ref, inverse_ref, forward_ref):
    for g in range(inverse_ref.shape[0]):
        forward_ref[g] = product(probe_ref[g], *split(inverse_ref[g]), NT)


def first(probes, inverses, chunk):
    blocks, rows, points = probes.shape[1], probes.shape[2] // CHUNKS, probes.shape[3]
    width = blocks // 2 if blocks % 2 == 0 else blocks
    return run(
        first_kernel,
        [jax.ShapeDtypeStruct((blocks, rows, points), F32)],
        (), [in_hbm(probes), in_hbm(inverses)],
        [
            pl.BlockSpec((None, width, rows, points), lambda g: (0, g, chunk, 0)),
            pl.BlockSpec((None, width, points, points), lambda g: (0, g, 0, 0)),
        ],
        grid=(blocks // width,),
        out_specs=[pl.BlockSpec((width, rows, points), lambda g: (g, 0, 0))],
    )[0]


def pack_kernel(asked_ref, *refs, base, whole, listed):
    sources, targets = refs[: 2 * len(whole)], refs[2 * len(whole) :]
    row = 0
    for target, offsets in zip(targets, (whole, listed, listed)):
        for place, offset in enumerate(offsets):
            held = whole.index(offset if offsets is whole else offset ^ 1)
            for core in range(2):
                for rank in range(CAP):
                    slot = jnp.maximum(asked_ref[base + row * CAP + rank], 0)
                    target[(place * 2 + core) * CAP + rank] = sources[held * 2 + core][slot]
                row += 1


def pack(asked, base, held, whole, listed):
    rows, points = held[0].shape[1:]
    return run(
        functools.partial(pack_kernel, base=base, whole=whole, listed=listed),
        [
            jax.ShapeDtypeStruct((len(offsets) * 2 * CAP, rows, points), F32)
            for offsets in (whole, listed, listed)
        ],
        (asked,), held,
    )


def gather_kernel(asked_ref, local_ref, *refs, base, whole, listed, blocks):
    sources, (keep_ref, give_ref) = refs[:3], refs[3:]
    for place in range(len(whole)):
        for core, target in enumerate((keep_ref, give_ref)):
            target[place] = local_ref[pl.ds((place * 2 + core) * blocks, blocks)]
    row = 0
    for source, offsets in zip(sources, (whole, listed, listed)):
        for place, offset in enumerate(offsets):
            held = whole.index(offset if offsets is whole else offset ^ 1)
            for core, target in enumerate((keep_ref, give_ref)):
                for rank in range(CAP):
                    slot = asked_ref[base + row * CAP + rank]
                    term = source[(place * 2 + core) * CAP + rank]

                    @pl.when(slot >= 0)
                    def _(target=target, held=held, slot=slot, term=term):
                        target[held, slot] = target[held, slot] + term

                row += 1


def gather_sums(asked, base, local, moved, whole, listed, blocks):
    rows, points = local.shape[1:]
    shape = jax.ShapeDtypeStruct((len(whole), blocks, rows, points), F32)
    return run(
        functools.partial(gather_kernel, base=base, whole=whole, listed=listed, blocks=blocks),
        [shape, shape], (asked,), [local, *moved],
    )


def add_kernel(first_ref, second_ref, *targets):
    for place, target in enumerate(targets, 1):
        target[...] = first_ref[place] + second_ref[place]


def add(kept, given):
    shape = jax.ShapeDtypeStruct(kept.shape[1:], F32)
    return run(add_kernel, [shape] * (kept.shape[0] - 1), (), [kept, given])


def solve_kernel(
    place_ref, panel_ref, *refs, has_fetch, has_left, has_parts, base, level, chunk, whole, listed, blocks, fanout, adds
):
    refs = list(refs)

    def take(count):
        taken, refs[:count] = refs[:count], []
        return taken

    inverse_refs = take(2)
    coupling_refs = take(2) if has_fetch or has_parts else None
    near_refs = take(2 * len(whole)) if has_fetch else []
    far_refs = take(3) if has_fetch else []
    sum_refs = take(2 + adds) if not has_fetch else []
    (out_ref,) = take(1)
    part_refs = take(4) if has_parts else []
    pan_ref = take(1)[0] if has_fetch else None
    hold_ref = take(1)[0] if has_parts else None
    rows = out_ref.shape[1]
    start = 0
    for ref in near_refs + far_refs:
        pan_ref[pl.ds(start, ref.shape[0])] = ref[...]
        start += ref.shape[0]
    if has_parts:
        hold_ref[...] = jnp.zeros(hold_ref.shape, F32)
    for g in range(blocks):
        inverse = [ref[level * blocks + g] for ref in inverse_refs]
        if has_fetch:
            value = panel_ref[level, g, pl.ds(chunk * rows, rows)]
            for k in range(fanout):
                coupling = [ref[g * fanout + k] for ref in coupling_refs]
                value = value - product(pan_ref[place_ref[base + g * fanout + k]], *coupling, NT)
            value = product(value, *inverse, NT)
        else:
            value = panel_ref[g] - sum_refs[0][0, g] - sum_refs[1][0, g]
            for ref in sum_refs[2:]:
                value = value - ref[g]
        if has_left:
            value = product(value, *inverse, NN)
        out_ref[g] = value
        if has_parts:
            for k in range(fanout):
                coupling = [ref[g * fanout + k] for ref in coupling_refs]
                at = place_ref[base + g * fanout + k]
                hold_ref[at] = hold_ref[at] + product(value, *coupling, NN)
    start = 0
    for ref in part_refs:
        ref[...] = hold_ref[pl.ds(start, ref.shape[0])]
        start += ref.shape[0]


def solve(
    places, base, panel, rows, level, chunk, inverse, coupling, whole, listed, blocks,
    near=None, far=None, sums=None, left=False,
):
    points = panel.shape[-1]
    has_fetch = near is not None
    has_parts = left and coupling is not None
    fanout = coupling[0].shape[0] // blocks if coupling is not None else 0
    operands = [panel, *[in_vmem(array) for array in [*inverse, *(coupling if coupling is not None else [])]]]
    operands += [*near, *far] if has_fetch else sums
    out_shapes = [jax.ShapeDtypeStruct((blocks, rows, points), F32)]
    sizes = [len(whole) * 2 * blocks, len(whole) * 2 * CAP, len(listed) * 2 * CAP, len(listed) * 2 * CAP]
    scratch = [pltpu.VMEM((sum(sizes), rows, points), F32)] * (has_fetch + has_parts)
    if has_parts:
        out_shapes += [jax.ShapeDtypeStruct((size, rows, points), F32) for size in sizes]
    kernel = functools.partial(
        solve_kernel, has_fetch=has_fetch, has_left=left, has_parts=has_parts, base=base, level=level, chunk=chunk,
        whole=whole, listed=listed, blocks=blocks, fanout=fanout, adds=0 if has_fetch else len(sums) - 2,
    )
    results = run(kernel, out_shapes, (places,), operands, scratch=scratch)
    return results[0], results[1:]


def place_kernel(*refs, spots, count):
    sources, target, sems = refs[: len(spots)], refs[count], refs[count + 1]
    copies = []
    for index, (source, (level, chunk)) in enumerate(zip(sources, spots)):
        rows = source.shape[1]
        goal = target.at[level, :, pl.ds(chunk * rows, rows)]
        copies.append(pltpu.make_async_copy(source, goal, sems.at[index]))
        copies[-1].start()
    for copy in copies:
        copy.wait()


def place(pieces, shape, target=None):
    operands = [*pieces.values(), *([] if target is None else [target])]
    return pl.pallas_call(
        functools.partial(place_kernel, spots=tuple(pieces), count=len(operands)),
        out_shape=pltpu.HBM(shape, F32),
        in_specs=[ANY_SPEC] * len(operands),
        out_specs=ANY_SPEC,
        scratch_shapes=[pltpu.SemaphoreType.DMA((len(pieces),))],
        input_output_aliases={} if target is None else {len(pieces): 0},
        compiler_params=PARAMS,
    )(*operands)


def flip_move(array, bits):
    members = lax.axis_size("blk")
    return lax.ppermute(array, "blk", [(source, source ^ bits) for source in range(members)])


def local(probes, inverses, couplings, neighbour_devices, neighbour_slots):
    members = lax.axis_size("blk")
    position = lax.axis_index("blk")
    blocks, fanout = probes.shape[1], couplings.shape[2]
    rows = probes.shape[2] // CHUNKS
    depth = members // LINE
    whole, listed = line_offsets(depth)
    asked, places = tables(neighbour_devices, neighbour_slots, members, position)
    asked_size, place_size = asked.shape[0] // (LEVELS - 1), places.shape[0] // (LEVELS - 1)
    travel = sorted(whole[1:], key=lambda offset: (offset.bit_count(), -offset))
    shared, ahead = {}, {}
    columns = [None] * CHUNKS

    def chain(chunk):
        call = functools.partial(
            solve, places, rows=rows, chunk=chunk, whole=whole, listed=listed, blocks=blocks
        )
        forward = [first(probes, inverses, chunk)]
        solved = [None] * LEVELS
        parts = None
        for level in range(1, LEVELS):
            held = {0: forward[-1]}
            for offset in travel:
                bit = low_bit(offset)
                held[offset] = flip_move(held[offset ^ bit], bit * LINE)
            near = []
            for offset in whole:
                swapped = held[offset]
                if offset and (level, chunk - 1) in ahead:
                    swapped, _ = lax.optimization_barrier((swapped, ahead[level, chunk - 1]))
                near += [held[offset], flip_move(swapped, CORE)]
            packs = pack(asked, (level - 1) * asked_size, near, whole, listed)
            if level in STAGGERED:
                ahead[level, chunk] = packs[0]
            far = [flip_move(array, bits) for array, bits in zip(packs, (SIDE, LINE, LINE | SIDE))]
            yield
            result, parts = call(
                base=(level - 1) * place_size, panel=shared["probes"], level=level, inverse=shared["inverse"],
                coupling=shared["coupling"][level - 1], near=near, far=far, left=level == LEVELS - 1,
            )
            forward.append(result)
        solved[LEVELS - 1] = forward.pop()
        for level in range(LEVELS - 2, -1, -1):
            moved = [flip_move(array, bits) for array, bits in zip(parts[1:], (SIDE, LINE, LINE | SIDE))]
            yield
            kept, gift = gather_sums(asked, level * asked_size, parts[0], moved, whole, listed, blocks)
            given = flip_move(gift, CORE)
            yield
            totals = dict(zip(whole[1:], add(kept, given)))
            addends = []
            for offset in travel[::-1]:
                bit = low_bit(offset)
                arrived = flip_move(totals[offset], bit * LINE)
                if offset == bit:
                    addends.append(arrived)
                else:
                    totals[offset ^ bit] = totals[offset ^ bit] + arrived
            yield
            solved[level], parts = call(
                base=max(level - 1, 0) * place_size, panel=forward[level], level=level, inverse=shared["inverse"],
                coupling=shared["coupling"][level - 1] if level else None, sums=[kept, given, *addends], left=True,
            )
        columns[chunk] = solved
        yield

    def prepare_couplings(level):
        shared.setdefault("coupling", {})[level] = halves(couplings, level, 4, max(1, blocks * fanout // 12))

    def prepare_inverses():
        every = inverses.reshape(1, -1, *inverses.shape[2:])
        shared["inverse"] = halves(every, 0, 3, blocks // 2 if blocks % 2 == 0 else blocks)
        shared["probes"] = probes

    chains = [chain(chunk) for chunk in range(CHUNKS)]
    for stage in range(4 * LEVELS):
        if stage == 1:
            prepare_inverses()
            for level in range(LEVELS - 1):
                prepare_couplings(level)
        for steps in chains:
            next(steps, None)
    pieces = {(level, chunk): columns[chunk][level] for chunk in range(CHUNKS) for level in range(LEVELS)}
    output = place({spot: array for spot, array in pieces.items() if spot[0]}, probes.shape)
    for chunk in range(CHUNKS):
        output = place({(0, chunk): pieces[0, chunk]}, probes.shape, output)
    return output


def solution(mesh):
    return jax.shard_map(
        local,
        mesh=mesh,
        in_specs=(
            P(None, ("grp", "blk"), None, None),
            P(None, ("grp", "blk"), None, None),
            P(None, ("grp", "blk"), None, None, None),
            P(None, "grp", None),
            P(None, "grp", None),
        ),
        out_specs=P(None, ("grp", "blk"), None, None),
        check_vma=False,
    )
```

```python
import functools

import jax
import jax.numpy as jnp
from jax import lax
from jax.experimental import pallas as pl
from jax.experimental.pallas import tpu as pltpu
from jax.sharding import PartitionSpec as P

LEVELS = 3
CAP = 2
CHUNKS = 2
STAGGERED = (1,)
CORE, SIDE, LINE = 1, 2, 4
F32 = jnp.float32
BF16 = jnp.bfloat16
NT = (((1,), (1,)), ((), ()))
NN = (((1,), (0,)), ((), ()))
PARAMS = pltpu.CompilerParams(vmem_limit_bytes=20 * 1024 * 1024)
VMEM_SPEC = pl.BlockSpec(memory_space=pltpu.VMEM)
ANY_SPEC = pl.BlockSpec(memory_space=pl.ANY)


def low_bit(offset):
    return offset & -offset


def in_hbm(array):
    return pltpu.with_memory_space_constraint(array, pltpu.HBM)


def in_vmem(array):
    return pltpu.with_memory_space_constraint(array, pltpu.VMEM)


def split(value):
    high = value.astype(BF16)
    return high, (value - high.astype(F32)).astype(BF16)


def product(panel, high, low, dims):
    rows = panel.shape[0]
    panel_high, panel_low = split(panel)
    both = lax.dot_general(
        jnp.concatenate([panel_high, panel_low], axis=0), high, dims, preferred_element_type=F32
    )
    cross = lax.dot_general(panel_high, low, dims, preferred_element_type=F32)
    return both[:rows] + (both[rows:] + cross)


def line_offsets(depth):
    whole = tuple(offset for offset in range(depth) if offset % 2 == 0 or offset == 1)
    return whole, tuple(offset for offset in range(depth) if offset not in whole)


def lookup(values, index):
    hits = index[..., None] == jnp.arange(len(values))
    return jnp.sum(jnp.where(hits, jnp.array(values, jnp.int32), 0), axis=-1)


def tables(dev_rows, slot_rows, members, position):
    levels, rows, fanout = dev_rows.shape
    blocks_dev = rows // members
    width = blocks_dev * fanout
    depth = members // LINE
    whole, listed = line_offsets(depth)
    height, place = position // LINE, position % LINE

    readers = jnp.stack([position, position ^ SIDE, position ^ LINE, position ^ (LINE | SIDE)])
    lists = jnp.take(dev_rows.reshape(levels, members, width), readers, axis=1)
    slots = jnp.take(slot_rows.reshape(levels, members, width), readers, axis=1)
    positions = jnp.arange(width)
    earlier = positions[None, :] < positions[:, None]
    matches = lists[..., :, None] == lists[..., None, :]
    rank = jnp.sum(jnp.logical_and(matches, earlier), axis=-1, dtype=jnp.int32)
    code = lists * CAP + rank

    def asked(reader, offsets):
        owners = (height ^ jnp.array(offsets, jnp.int32))[:, None] * LINE + (place ^ jnp.arange(2))[None, :]
        wanted = (owners[..., None] * CAP + jnp.arange(CAP)).reshape(-1)
        found = code[:, reader, None, :] == wanted[None, :, None]
        return jnp.sum(jnp.where(found, slots[:, reader, None, :] + 1, 0), axis=2) - 1

    across = tuple(offset ^ 1 for offset in listed)
    table = jnp.concatenate([asked(1, whole), asked(2, across), asked(3, across)], axis=1)
    own_dev, own_slot, own_rank = lists[:, 0], slots[:, 0], rank[:, 0]
    flip = (own_dev % LINE) ^ place
    side, core = flip // SIDE, flip % SIDE
    offset = (own_dev // LINE) ^ height
    spot = lookup([whole.index(o) if o in whole else listed.index(o) for o in range(depth)], offset)
    is_whole = lookup([int(o in whole) for o in range(depth)], offset) == 1
    at_side = len(whole) * 2 * blocks_dev
    at_far = at_side + len(whole) * 2 * CAP
    place_of = jnp.where(
        is_whole,
        jnp.where(
            side == 0,
            (spot * 2 + core) * blocks_dev + own_slot,
            at_side + (spot * 2 + core) * CAP + own_rank,
        ),
        at_far + ((side * len(listed) + spot) * 2 + core) * CAP + own_rank,
    )
    return table.reshape(-1), place_of.reshape(-1)


COST = pl.CostEstimate(flops=600_000_000, bytes_accessed=3_000_000, transcendentals=0)


def run(kernel, out_shape, tables, operands, specs=None, scratch=(), grid=(), out_specs=None):
    return pl.pallas_call(
        kernel,
        out_shape=out_shape,
        grid_spec=pltpu.PrefetchScalarGridSpec(
            num_scalar_prefetch=len(tables),
            grid=grid,
            in_specs=specs if specs is not None else [VMEM_SPEC] * len(operands),
            out_specs=out_specs if out_specs is not None else [VMEM_SPEC] * len(out_shape),
            scratch_shapes=list(scratch),
        ),
        compiler_params=PARAMS,
        cost_estimate=COST,
    )(*tables, *operands)


def halves_kernel(*refs, streams, count):
    step = pl.program_id(0)
    for stream in range(streams):
        high, low = split(refs[stream][...])
        at = pl.ds((stream * count + step) * high.shape[0], high.shape[0])
        refs[streams][at], refs[streams + 1][at] = high, low


def halves(matrices, level, streams, width):
    points = matrices.shape[-1]
    matrices = matrices.reshape(matrices.shape[0], -1, points, points)
    total = matrices.shape[1]
    count = total // (streams * width)
    shape = pltpu.VMEM((total, points, points), BF16)
    specs = [
        pl.BlockSpec((None, width, points, points), lambda step, stream=stream: (level, stream * count + step, 0, 0))
        for stream in range(streams)
    ]
    return run(
        functools.partial(halves_kernel, streams=streams, count=count),
        [shape, shape], (), [in_hbm(matrices)] * streams, specs, grid=(count,),
    )


def first_kernel(probe_ref, inverse_ref, forward_ref):
    for g in range(inverse_ref.shape[0]):
        forward_ref[g] = product(probe_ref[g], *split(inverse_ref[g]), NT)


def first(probes, inverses, chunk):
    blocks, rows, points = probes.shape[1], probes.shape[2] // CHUNKS, probes.shape[3]
    width = blocks // 2 if blocks % 2 == 0 else blocks
    return run(
        first_kernel,
        [jax.ShapeDtypeStruct((blocks, rows, points), F32)],
        (), [in_hbm(probes), in_hbm(inverses)],
        [
            pl.BlockSpec((None, width, rows, points), lambda g: (0, g, chunk, 0)),
            pl.BlockSpec((None, width, points, points), lambda g: (0, g, 0, 0)),
        ],
        grid=(blocks // width,),
        out_specs=[pl.BlockSpec((width, rows, points), lambda g: (g, 0, 0))],
    )[0]


def pack_kernel(asked_ref, *refs, base, whole, listed):
    sources, targets = refs[: 2 * len(whole)], refs[2 * len(whole) :]
    row = 0
    for target, offsets in zip(targets, (whole, listed, listed)):
        for place, offset in enumerate(offsets):
            held = whole.index(offset if offsets is whole else offset ^ 1)
            for core in range(2):
                for rank in range(CAP):
                    slot = jnp.maximum(asked_ref[base + row * CAP + rank], 0)
                    target[(place * 2 + core) * CAP + rank] = sources[held * 2 + core][slot]
                row += 1


def pack(asked, base, held, whole, listed):
    rows, points = held[0].shape[1:]
    return run(
        functools.partial(pack_kernel, base=base, whole=whole, listed=listed),
        [
            jax.ShapeDtypeStruct((len(offsets) * 2 * CAP, rows, points), F32)
            for offsets in (whole, listed, listed)
        ],
        (asked,), held,
    )


def gather_kernel(asked_ref, local_ref, *refs, base, whole, listed, blocks):
    sources, (keep_ref, give_ref) = refs[:3], refs[3:]
    for place in range(len(whole)):
        for core, target in enumerate((keep_ref, give_ref)):
            target[place] = local_ref[pl.ds((place * 2 + core) * blocks, blocks)]
    row = 0
    for source, offsets in zip(sources, (whole, listed, listed)):
        for place, offset in enumerate(offsets):
            held = whole.index(offset if offsets is whole else offset ^ 1)
            for core, target in enumerate((keep_ref, give_ref)):
                for rank in range(CAP):
                    slot = asked_ref[base + row * CAP + rank]
                    term = source[(place * 2 + core) * CAP + rank]

                    @pl.when(slot >= 0)
                    def _(target=target, held=held, slot=slot, term=term):
                        target[held, slot] = target[held, slot] + term

                row += 1


def gather_sums(asked, base, local, moved, whole, listed, blocks):
    rows, points = local.shape[1:]
    shape = jax.ShapeDtypeStruct((len(whole), blocks, rows, points), F32)
    return run(
        functools.partial(gather_kernel, base=base, whole=whole, listed=listed, blocks=blocks),
        [shape, shape], (asked,), [local, *moved],
    )


def add_kernel(first_ref, second_ref, *targets):
    for place, target in enumerate(targets, 1):
        target[...] = first_ref[place] + second_ref[place]


def add(kept, given):
    shape = jax.ShapeDtypeStruct(kept.shape[1:], F32)
    return run(add_kernel, [shape] * (kept.shape[0] - 1), (), [kept, given])


def solve_kernel(
    place_ref, panel_ref, *refs, has_fetch, has_left, has_parts, base, level, chunk, whole, listed, blocks, fanout, adds
):
    refs = list(refs)

    def take(count):
        taken, refs[:count] = refs[:count], []
        return taken

    inverse_refs = take(2)
    coupling_refs = take(2) if has_fetch or has_parts else None
    near_refs = take(2 * len(whole)) if has_fetch else []
    far_refs = take(3) if has_fetch else []
    sum_refs = take(2 + adds) if not has_fetch else []
    (out_ref,) = take(1)
    part_refs = take(4) if has_parts else []
    pan_ref = take(1)[0] if has_fetch else None
    hold_ref = take(1)[0] if has_parts else None
    rows = out_ref.shape[1]
    start = 0
    for ref in near_refs + far_refs:
        pan_ref[pl.ds(start, ref.shape[0])] = ref[...]
        start += ref.shape[0]
    if has_parts:
        hold_ref[...] = jnp.zeros(hold_ref.shape, F32)
    for g in range(blocks):
        inverse = [ref[level * blocks + g] for ref in inverse_refs]
        if has_fetch:
            value = panel_ref[level, g, pl.ds(chunk * rows, rows)]
            for k in range(fanout):
                coupling = [ref[g * fanout + k] for ref in coupling_refs]
                value = value - product(pan_ref[place_ref[base + g * fanout + k]], *coupling, NT)
            value = product(value, *inverse, NT)
        else:
            value = panel_ref[g] - sum_refs[0][0, g] - sum_refs[1][0, g]
            for ref in sum_refs[2:]:
                value = value - ref[g]
        if has_left:
            value = product(value, *inverse, NN)
        out_ref[g] = value
        if has_parts:
            for k in range(fanout):
                coupling = [ref[g * fanout + k] for ref in coupling_refs]
                at = place_ref[base + g * fanout + k]
                hold_ref[at] = hold_ref[at] + product(value, *coupling, NN)
    start = 0
    for ref in part_refs:
        ref[...] = hold_ref[pl.ds(start, ref.shape[0])]
        start += ref.shape[0]


def solve(
    places, base, panel, rows, level, chunk, inverse, coupling, whole, listed, blocks,
    near=None, far=None, sums=None, left=False,
):
    points = panel.shape[-1]
    has_fetch = near is not None
    has_parts = left and coupling is not None
    fanout = coupling[0].shape[0] // blocks if coupling is not None else 0
    operands = [panel, *[in_vmem(array) for array in [*inverse, *(coupling if coupling is not None else [])]]]
    operands += [*near, *far] if has_fetch else sums
    out_shapes = [jax.ShapeDtypeStruct((blocks, rows, points), F32)]
    sizes = [len(whole) * 2 * blocks, len(whole) * 2 * CAP, len(listed) * 2 * CAP, len(listed) * 2 * CAP]
    scratch = [pltpu.VMEM((sum(sizes), rows, points), F32)] * (has_fetch + has_parts)
    if has_parts:
        out_shapes += [jax.ShapeDtypeStruct((size, rows, points), F32) for size in sizes]
    kernel = functools.partial(
        solve_kernel, has_fetch=has_fetch, has_left=left, has_parts=has_parts, base=base, level=level, chunk=chunk,
        whole=whole, listed=listed, blocks=blocks, fanout=fanout, adds=0 if has_fetch else len(sums) - 2,
    )
    results = run(kernel, out_shapes, (places,), operands, scratch=scratch)
    return results[0], results[1:]


def place_kernel(*refs, spots, count):
    sources, target, sems = refs[: len(spots)], refs[count], refs[count + 1]
    copies = []
    for index, (source, (level, chunk)) in enumerate(zip(sources, spots)):
        rows = source.shape[1]
        goal = target.at[level, :, pl.ds(chunk * rows, rows)]
        copies.append(pltpu.make_async_copy(source, goal, sems.at[index]))
        copies[-1].start()
    for copy in copies:
        copy.wait()


def place(pieces, shape, target=None):
    operands = [*pieces.values(), *([] if target is None else [target])]
    return pl.pallas_call(
        functools.partial(place_kernel, spots=tuple(pieces), count=len(operands)),
        out_shape=pltpu.HBM(shape, F32),
        in_specs=[ANY_SPEC] * len(operands),
        out_specs=ANY_SPEC,
        scratch_shapes=[pltpu.SemaphoreType.DMA((len(pieces),))],
        input_output_aliases={} if target is None else {len(pieces): 0},
        compiler_params=PARAMS,
    )(*operands)


def flip_move(array, bits):
    members = lax.axis_size("blk")
    return lax.ppermute(array, "blk", [(source, source ^ bits) for source in range(members)])


def local(probes, inverses, couplings, neighbour_devices, neighbour_slots):
    members = lax.axis_size("blk")
    position = lax.axis_index("blk")
    blocks, fanout = probes.shape[1], couplings.shape[2]
    rows = probes.shape[2] // CHUNKS
    depth = members // LINE
    whole, listed = line_offsets(depth)
    asked, places = tables(neighbour_devices, neighbour_slots, members, position)
    asked_size, place_size = asked.shape[0] // (LEVELS - 1), places.shape[0] // (LEVELS - 1)
    travel = sorted(whole[1:], key=lambda offset: (offset.bit_count(), offset))
    shared, ahead = {}, {}
    columns = [None] * CHUNKS

    def chain(chunk):
        call = functools.partial(
            solve, places, rows=rows, chunk=chunk, whole=whole, listed=listed, blocks=blocks
        )
        forward = [first(probes, inverses, chunk)]
        solved = [None] * LEVELS
        parts = None
        for level in range(1, LEVELS):
            held = {0: forward[-1]}
            for offset in travel:
                bit = low_bit(offset)
                held[offset] = flip_move(held[offset ^ bit], bit * LINE)
            near = []
            for offset in whole:
                swapped = held[offset]
                if offset and (level, chunk - 1) in ahead:
                    swapped, _ = lax.optimization_barrier((swapped, ahead[level, chunk - 1]))
                near += [held[offset], flip_move(swapped, CORE)]
            packs = pack(asked, (level - 1) * asked_size, near, whole, listed)
            if level in STAGGERED:
                ahead[level, chunk] = packs[0]
            far = [flip_move(array, bits) for array, bits in zip(packs, (SIDE, LINE, LINE | SIDE))]
            yield
            result, parts = call(
                base=(level - 1) * place_size, panel=shared["probes"], level=level, inverse=shared["inverse"],
                coupling=shared["coupling"][level - 1], near=near, far=far, left=level == LEVELS - 1,
            )
            forward.append(result)
        solved[LEVELS - 1] = forward.pop()
        for level in range(LEVELS - 2, -1, -1):
            moved = [flip_move(array, bits) for array, bits in zip(parts[1:], (SIDE, LINE, LINE | SIDE))]
            yield
            kept, gift = gather_sums(asked, level * asked_size, parts[0], moved, whole, listed, blocks)
            given = flip_move(gift, CORE)
            yield
            totals = dict(zip(whole[1:], add(kept, given)))
            addends = []
            for offset in travel[::-1]:
                bit = low_bit(offset)
                arrived = flip_move(totals[offset], bit * LINE)
                if offset == bit:
                    addends.append(arrived)
                else:
                    totals[offset ^ bit] = totals[offset ^ bit] + arrived
            yield
            solved[level], parts = call(
                base=max(level - 1, 0) * place_size, panel=forward[level], level=level, inverse=shared["inverse"],
                coupling=shared["coupling"][level - 1] if level else None, sums=[kept, given, *addends], left=True,
            )
        columns[chunk] = solved
        yield

    def prepare_couplings(level):
        shared.setdefault("coupling", {})[level] = halves(couplings, level, 4, max(1, blocks * fanout // 12))

    def prepare_inverses():
        every = inverses.reshape(1, -1, *inverses.shape[2:])
        shared["inverse"] = halves(every, 0, 3, blocks // 2 if blocks % 2 == 0 else blocks)
        shared["probes"] = probes

    chains = [chain(chunk) for chunk in range(CHUNKS)]
    for stage in range(4 * LEVELS):
        if stage == 1:
            prepare_inverses()
            for level in range(LEVELS - 1):
                prepare_couplings(level)
        for steps in chains:
            next(steps, None)
    pieces = {(level, chunk): columns[chunk][level] for chunk in range(CHUNKS) for level in range(LEVELS)}
    output = place({spot: array for spot, array in pieces.items() if spot[0]}, probes.shape)
    for chunk in range(CHUNKS):
        output = place({(0, chunk): pieces[0, chunk]}, probes.shape, output)
    return output


def solution(mesh):
    return jax.shard_map(
        local,
        mesh=mesh,
        in_specs=(
            P(None, ("grp", "blk"), None, None),
            P(None, ("grp", "blk"), None, None),
            P(None, ("grp", "blk"), None, None, None),
            P(None, "grp", None),
            P(None, "grp", None),
        ),
        out_specs=P(None, ("grp", "blk"), None, None),
        check_vma=False,
    )
```
